32 devices in a mesh: row: 8 (over z, core), col: 4 (over y, x).
Axes of the slice: x: 2, y: 2, z: 4, core: 2. Of those that a mesh axis runs over, the one named last changes fastest.
Arguments:
- object_slices: float32 [2, 2, 2048, 1024], P(None, None, 'row', 'col'), may hold values from -5 to 5
- probe_wave: float32 [2, 256, 256], replicated, may hold values from -6 to 6
- propagator: float32 [2, 256, 256], replicated, may hold values from -5 to 5
- measured: float32 [8, 4, 4, 256, 256], P('row', 'col'), as said below
- positions: int32 [8, 4, 4, 2], P('row', 'col'), may hold values from -128 to 128, as said below
- scan_counts: int32 [8, 4], P('row', 'col'), may hold values from 1 to 4, as said below
Outputs:
- object_grad: float32 [2, 2, 2048, 1024], P(None, None, 'row', 'col')
- probe_grad: float32 [2, 256, 256], replicated
The draws below stay inside these ranges and needn't reach their ends.
Inputs may be any that keep to these rules, and one draw needn't show every extreme that they name: `positions`: every patch of 256 x 256 cells lies inside the object window. Slots k < scan_counts[r, c] of tile (r, c) are used, the others are ignored. `measured`: positive intensities.
All inputs are finite; a program needn't handle non-finite values.
Results may differ from the reference program's by a relative error of at most 0.0003.
Values sent between devices are 32-bit elements; how exact they have to be, the bound alone decides.
No kernel may reach another device: no remote copies, remote signals or barrier semaphores. Data moves between devices by JAX's collectives and lax.ppermute only.
A program may use at most 128 MiB of HBM per device.

```python
import math
import jax
import jax.numpy as jnp
from jax import lax

W = 256
HALF = 128
SLICES = 2
TILE = 256
CAP = 4
NTR = 8
NTC = 4
OY = 2048
OX = 1024


def draw_scan_counts(key, part):
    key = jax.random.fold_in(key, 12)
    first_key, second_key, third_key = jax.random.split(key, 3)
    first = jax.random.randint(first_key, (NTR, NTC), 1, CAP + 1)
    second = jax.random.randint(second_key, (NTR, NTC), 1, CAP + 1)
    counted = jnp.minimum(first, second).reshape(-1)
    chosen = jax.random.randint(third_key, (), 0, NTR * NTC)
    counted = jnp.where(jnp.arange(NTR * NTC) == chosen, CAP, counted)
    return counted.reshape(NTR, NTC).astype(jnp.int32)


def draw_positions(key, part):
    key = jax.random.fold_in(key, 13)
    row_key, col_key = jax.random.split(key, 2)
    tile_row = jnp.arange(NTR, dtype=jnp.int32)[:, None, None]
    tile_col = jnp.arange(NTC, dtype=jnp.int32)[None, :, None]
    slot_at = jnp.arange(CAP, dtype=jnp.int32)[None, None, :]
    row_low = jnp.where(tile_row > 0, 0 - HALF, 0)
    row_high = jnp.where(tile_row < NTR - 1, TILE - HALF, TILE - W)
    col_low = jnp.where(tile_col > 0, 0 - HALF, 0)
    col_high = jnp.where(tile_col < NTC - 1, TILE - HALF, TILE - W)
    row_draw = jax.random.randint(row_key, (NTR, NTC, CAP), 0, 1 << 20)
    col_draw = jax.random.randint(col_key, (NTR, NTC, CAP), 0, 1 << 20)
    rows = row_low + row_draw % (row_high - row_low + 1)
    cols = col_low + col_draw % (col_high - col_low + 1)
    even = (tile_row + tile_col) % 2 == 0
    rows = jnp.where(slot_at == 0, jnp.where(even, row_low, row_high), rows)
    cols = jnp.where(slot_at == 0, jnp.where(even, col_high, col_low), cols)
    return jnp.stack((rows, cols), axis=-1).astype(jnp.int32)


def draw_measured(key, part):
    key = jax.random.fold_in(key, 14)
    pixel_key, pattern_key = jax.random.split(key, 2)
    tile_rows = jnp.arange(NTR, dtype=jnp.float32)[:, None, None, None, None]
    tile_scale = 1.0 + 2.0 * tile_rows / max(NTR - 1, 1)
    pattern = jnp.exp(jax.random.uniform(pattern_key, (NTR, NTC, CAP, 1, 1), dtype=jnp.float32) * math.log(10.0))
    pixels = jax.random.uniform(pixel_key, (NTR, NTC, CAP, W, W), dtype=jnp.float32, minval=0.2, maxval=2.0)
    return (tile_scale * pattern * pixels).astype(jnp.float32)


def steps_of(own_key, shape, cuts, low, top_value):
    def one(axis_at, parts):
        steps = jax.random.uniform(jax.random.fold_in(jax.random.fold_in(own_key, 6), axis_at), (parts,), jnp.float32, low / len(cuts), top_value / len(cuts))
        return jnp.repeat(jnp.exp(steps), shape[axis_at] // parts).reshape((-1,) + (1,) * (len(shape) - axis_at - 1))

    factor_of = one(*cuts[0])
    for cut in cuts[1:]:
        factor_of = factor_of * one(*cut)
    return factor_of


def normal_values(own_key, extent, scale, limit, cuts=(), kind=jnp.bfloat16):
    drawn = scale * jax.random.normal(own_key, extent, jnp.float32)
    if cuts:
        drawn = drawn * steps_of(own_key, extent, cuts, -0.22, 0.18)
    return jnp.clip(drawn, -limit, limit).astype(kind)


def setup_inputs(seed: int = 0) -> dict:
    splits = jax.random.split(jax.random.key(seed), 7)
    object_slices = normal_values(splits[0], (SLICES, 2, OY, OX), 0.7, 5.0, ((2, 8), (3, 4)), jnp.float32)
    probe_wave = normal_values(splits[1], (2, W, W), 1.0, 6.0, (), jnp.float32)
    propagator = normal_values(splits[2], (2, W, W), 0.7, 5.0, (), jnp.float32)
    measured = draw_measured(jax.random.fold_in(splits[6], 71), 0)
    positions = draw_positions(jax.random.fold_in(splits[6], 71), 0)
    scan_counts = draw_scan_counts(jax.random.fold_in(splits[6], 71), 0)
    return {"object_slices": object_slices, "probe_wave": probe_wave, "propagator": propagator, "measured": measured, "positions": positions, "scan_counts": scan_counts}


def forward_fft(field):
    return jnp.fft.fft2(field, norm="ortho")


def inverse_fft(field):
    return jnp.fft.ifft2(field, norm="ortho")


def slot_gradient(patch, probe_wave, propagator, target):
    kernel = lax.complex(propagator[0], propagator[1])
    wave = lax.complex(probe_wave[0], probe_wave[1])
    layers = patch.shape[0]
    incoming = []
    transmits = []
    for layer_at in range(layers):
        transmit = lax.complex(patch[layer_at, 0], patch[layer_at, 1])
        transmits.append(transmit)
        incoming.append(wave)
        exited = wave * transmit
        if layer_at + 1 < layers:
            wave = inverse_fft(kernel * forward_fft(exited))
    far_field = forward_fft(exited)
    misfit = jnp.real(far_field) * jnp.real(far_field) + jnp.imag(far_field) * jnp.imag(far_field) - target
    adjoint = inverse_fft(misfit * far_field)
    gradients = [None] * layers
    for layer_at in range(layers - 1, -1, -1):
        term = jnp.conj(incoming[layer_at]) * adjoint
        gradients[layer_at] = jnp.stack((jnp.real(term), jnp.imag(term)))
        adjoint = jnp.conj(transmits[layer_at]) * adjoint
        if layer_at > 0:
            adjoint = inverse_fft(jnp.conj(kernel) * forward_fft(adjoint))
    return jnp.stack(gradients), jnp.stack((jnp.real(adjoint), jnp.imag(adjoint)))


def reference(object_slices, probe_wave, propagator, measured, positions, scan_counts):
    float_type = object_slices.dtype
    padded = jnp.pad(object_slices, ((0, 0), (0, 0), (HALF, HALF), (HALF, HALF)))
    per_tile = NTC * CAP

    def visit(state_pair, flat_index):
        accum, probe_sum = state_pair
        tile_row = flat_index // per_tile
        tile_col = (flat_index // CAP) % NTC
        slot_at = flat_index % CAP
        offset = positions[tile_row, tile_col, slot_at]
        row_start = (tile_row * TILE + offset[0] + HALF).astype(jnp.int32)
        col_start = (tile_col * TILE + offset[1] + HALF).astype(jnp.int32)
        starts = (jnp.int32(0), jnp.int32(0), row_start, col_start)
        patch = lax.dynamic_slice(padded, starts, (SLICES, 2, W, W))
        gradients, adjoint = slot_gradient(patch, probe_wave, propagator, measured[tile_row, tile_col, slot_at])
        weight = (slot_at < scan_counts[tile_row, tile_col]).astype(float_type)
        region = lax.dynamic_slice(accum, starts, (SLICES, 2, W, W)) + weight * gradients
        accum = lax.dynamic_update_slice(accum, region, starts)
        return (accum, probe_sum + weight * adjoint), None

    initial = (jnp.zeros_like(padded), jnp.zeros((2, W, W), float_type))
    (accum, probe_sum), trailing = lax.scan(visit, initial, jnp.arange(NTR * NTC * CAP, dtype=jnp.int32))
    live = (jnp.arange(CAP, dtype=jnp.int32)[None, None, :] < scan_counts[:, :, None]).astype(float_type)
    total = jnp.sum(live * jnp.sum(measured, axis=(3, 4)))
    scans = jnp.sum(scan_counts).astype(float_type)
    mean_level = total / (scans * (W * W))
    object_grad = accum[:, :, HALF:HALF + OY, HALF:HALF + OX] / mean_level
    return object_grad, probe_sum / (mean_level * scans)
```

```python
import functools

import jax
import jax.numpy as jnp
import numpy as np
from jax import lax
from jax.experimental import pallas as pl
from jax.experimental.pallas import tpu as pltpu
from jax.sharding import PartitionSpec as P

F32 = jnp.float32
BF16 = jnp.bfloat16


def split_table(table):
    high = table.astype(BF16)
    low = (table - high.astype(np.float64)).astype(BF16)
    return high, low


@functools.lru_cache(None)
def tables(width):
    half = width // 2
    index = np.arange(half)
    angle = 2.0 * np.pi * ((index[:, None] * index[None, :]) % half) / half
    cosine, sine = np.cos(angle) / np.sqrt(width), np.sin(angle) / np.sqrt(width)
    first = split_table(np.block([[cosine, sine], [-sine, cosine]]))
    second = split_table(np.block([[cosine, -sine], [sine, cosine]]))
    turn = 2.0 * np.pi * index / width
    turns = np.stack([np.cos(turn), np.sin(turn)]).astype(np.float32)
    row = np.broadcast_to(turns[:, :, None], (2, half, half))
    lane = np.broadcast_to(turns[:, None, :], (2, 8, half))
    spread = np.zeros((width, width))
    spread[np.arange(width), index_order(width)] = 1.0
    matrices = [*first, *second, spread.astype(BF16), spread.T.astype(BF16)]
    return np.stack(matrices), np.concatenate([row, lane], axis=1)


def index_order(width):
    index = np.arange(width)
    return index // 2 + (index % 2) * (width // 2)


def split(value):
    high = value.astype(BF16)
    low = (value - high.astype(F32)).astype(BF16)
    return high, low


def right_dot(value, matrix):
    high, low = split(value)
    return jnp.dot(
        jnp.concatenate([high, low, high], axis=1),
        jnp.concatenate([matrix[0], matrix[0], matrix[1]], axis=0),
        preferred_element_type=F32,
    )


def left_dot(matrix, value):
    high, low = split(value)
    return jnp.dot(
        jnp.concatenate([matrix[0], matrix[0], matrix[1]], axis=1),
        jnp.concatenate([high, low, high], axis=0),
        preferred_element_type=F32,
    )


def mul(a, b):
    return a[0] * b[0] - a[1] * b[1], a[0] * b[1] + a[1] * b[0]


def conj_mul(a, b):
    return a[0] * b[0] + a[1] * b[1], a[0] * b[1] - a[1] * b[0]


def right_forward(field, lane, matrix):
    half = field[0].shape[1] // 2
    rows = field[0].shape[0]
    a = tuple(part[:, :half] for part in field)
    b = tuple(part[:, half:] for part in field)
    u = (a[0] + b[0], a[1] + b[1])
    v = conj_mul(lane, (a[0] - b[0], a[1] - b[1]))
    stacked = jnp.concatenate(
        [jnp.concatenate(u, axis=1), jnp.concatenate(v, axis=1)], axis=0
    )
    out = right_dot(stacked, matrix)
    even, odd = out[:rows], out[rows:]
    return (
        jnp.concatenate([even[:, :half], odd[:, :half]], axis=1),
        jnp.concatenate([even[:, half:], odd[:, half:]], axis=1),
    )


def right_inverse(field, lane, matrix):
    half = field[0].shape[1] // 2
    rows = field[0].shape[0]
    even = jnp.concatenate([field[0][:, :half], field[1][:, :half]], axis=1)
    odd = jnp.concatenate([field[0][:, half:], field[1][:, half:]], axis=1)
    out = right_dot(jnp.concatenate([even, odd], axis=0), matrix)
    even, odd = out[:rows], out[rows:]
    even = (even[:, :half], even[:, half:])
    odd = mul(lane, (odd[:, :half], odd[:, half:]))
    return tuple(
        jnp.concatenate([e + o, e - o], axis=1) for e, o in zip(even, odd)
    )


def left_pair(field, row, forward, inverse, middle):
    half = field[0].shape[0] // 2
    lanes = field[0].shape[1]
    a = tuple(part[:half] for part in field)
    b = tuple(part[half:] for part in field)
    u = (a[0] + b[0], a[1] + b[1])
    v = conj_mul(row, (a[0] - b[0], a[1] - b[1]))
    stacked = jnp.concatenate(
        [jnp.concatenate(u, axis=0), jnp.concatenate(v, axis=0)], axis=1
    )
    out = left_dot(forward, stacked)
    even = middle(0, (out[:half, :lanes], out[half:, :lanes]))
    odd = middle(1, (out[:half, lanes:], out[half:, lanes:]))
    stacked = jnp.concatenate(
        [jnp.concatenate(even, axis=0), jnp.concatenate(odd, axis=0)], axis=1
    )
    out = left_dot(inverse, stacked)
    even = (out[:half, :lanes], out[half:, :lanes])
    odd = mul(row, (out[:half, lanes:], out[half:, lanes:]))
    return tuple(
        jnp.concatenate([e + o, e - o], axis=0) for e, o in zip(even, odd)
    )


def lane_pair(turns):
    half = turns.shape[2]
    return turns[0, half : half + 1, :], turns[1, half : half + 1, :]


def left_stage(works, turns, forward, inverse, middles):
    half = turns.shape[2]
    for at in range(works[0].shape[2] // half):
        lanes = pl.ds(at * half, half)
        for work, middle in zip(works, middles):
            out = left_pair(
                (work[0, :, lanes], work[1, :, lanes]),
                (turns[0, :half, :], turns[1, :half, :]),
                forward,
                inverse,
                functools.partial(middle, lanes),
            )
            work[0, :, lanes] = out[0]
            work[1, :, lanes] = out[1]


def pair_of(count, at):
    both = 2 * at + 1 < count
    second = 2 * at + both.astype(jnp.int32)
    return (2 * at, 1.0), (second, both.astype(F32))


def device_bits():
    row, col = lax.axis_index("row"), lax.axis_index("col")
    return row & 1, col & 1, (row >> 1) & 1, (row >> 2) & 1


def other_end(parity, span):
    return pl.multiple_of((1 - parity) * span, 8), pl.multiple_of(parity * span, 8)


def assemble(ext, bits, tile, sides, strips):
    half = sides[0].shape[2]
    size = tile.shape[1]
    blocks = size // half
    for part in range(2):
        for at in range(blocks):
            ext[part, 1 + at, half : half + size, :] = tile[part, :, at * half : (at + 1) * half]
        for side, at in zip(sides, ((1 - bits[1]) * (blocks + 1), bits[1] * (blocks + 1))):
            ext[part, at, half : half + size, :] = side[part]
        for strip, start in zip(strips, other_end(bits[0], half + size)):
            for at in range(blocks + 2):
                ext[part, at, pl.ds(start, half), :] = strip[part, :, at * half : (at + 1) * half]


def place(positions, slot_at, half):
    row = positions[0, slot_at] + half
    col = positions[1, slot_at] + half
    return row, col // half, col % half


def read_patch(ext, part, row, rows, base, shift, half):
    blocks = []
    for at in range(3):
        block = ext[part, base + at, pl.ds(row, rows), :]
        blocks.append(pltpu.roll(block, lax.rem(half - shift, half), 1))
    own = lax.broadcasted_iota(jnp.int32, (rows, half), 1) < half - shift
    return jnp.concatenate(
        [jnp.where(own, blocks[0], blocks[1]), jnp.where(own, blocks[1], blocks[2])], axis=1
    )


def add_patch(acc, part, row, base, shift, value):
    rows, width = value.shape
    half = width // 2
    first = pltpu.roll(value[:, :half], shift, 1)
    second = pltpu.roll(value[:, half:], shift, 1)
    own = lax.broadcasted_iota(jnp.int32, (rows, half), 1) >= shift
    zero = jnp.zeros_like(first)
    blocks = (
        jnp.where(own, first, zero),
        jnp.where(own, second, first),
        jnp.where(own, zero, second),
    )
    for at, block in enumerate(blocks):
        spot = (part, base + at, pl.ds(row, rows), slice(None))
        acc[spot] = acc[spot] + block


def write_out(acc, bits, centre, strips):
    half = acc.shape[3]
    size = centre.shape[1]
    for part in range(2):
        for at in range(centre.shape[2] // half):
            lanes = slice(at * half, (at + 1) * half)
            centre[part, :, lanes] = acc[part, at, half : half + size, :]
            for strip, start in zip(strips, other_end(bits[0], half + size)):
                strip[part, :, lanes] = acc[part, at, pl.ds(start, half), :]


CHUNK = 128


def chunks(width):
    return range(0, width, CHUNK)


def three_parts(value):
    high = value.astype(BF16)
    rest = value - high.astype(F32)
    middle = rest.astype(BF16)
    return high, middle, (rest - middle.astype(F32)).astype(BF16)


def prepare_kernel(count, measured, propagator, matrices, targets, kernel_out, total):
    slots = measured.shape[0]

    def reorder(source, at, out):
        moved = jnp.dot(
            jnp.concatenate(three_parts(source[at]), axis=1),
            jnp.concatenate([matrices[4]] * 3, axis=0),
            preferred_element_type=F32,
        )
        out[at] = jnp.dot(
            jnp.concatenate([matrices[5]] * 3, axis=1),
            jnp.concatenate(three_parts(moved), axis=0),
            preferred_element_type=F32,
        )

    used = jnp.float32(0.0)
    for slot_at in range(slots):
        reorder(measured, slot_at, targets)
        sums = jnp.sum(measured[slot_at])
        used = used + jnp.where(slot_at < count[0, 0], sums, jnp.float32(0.0))
    for part in range(2):
        reorder(propagator, part, kernel_out)
    total[0, 0] = used


def first_kernel(
    count, positions, tiles, side_a, side_b, strip_a, strip_b, probe, transfer,
    turns, matrices,
    waves, patches, ext, work,
):
    width = probe.shape[1]
    half = width // 2
    assemble(ext, device_bits(), tiles.at[0], (side_a, side_b), (strip_a, strip_b))

    def through(lanes, parity, value):
        rows = pl.ds(parity * half, half)
        return mul((transfer[0, rows, lanes], transfer[1, rows, lanes]), value)

    first, second = matrices.at[0:2], matrices.at[2:4]

    def visit(pair_at, carry):
        slots = [slot for slot, weight in pair_of(count[0, 0], pair_at)]
        places = [place(positions, slot, half) for slot in slots]
        works = [work.at[at] for at in range(2)]
        turn = lane_pair(turns)
        for at in chunks(width):
            rows = pl.ds(at, CHUNK)
            for slot, (row, base, shift), field in zip(slots, places, works):
                patch = tuple(
                    read_patch(ext, part, row + at, CHUNK, base, shift, half) for part in range(2)
                )
                for part in range(2):
                    patches[slot, part, rows, :] = patch[part]
                exited = mul((probe[0, rows, :], probe[1, rows, :]), patch)
                out = right_forward(exited, turn, second)
                field[0, rows, :] = out[0]
                field[1, rows, :] = out[1]
        left_stage(works, turns, first, second, [through] * 2)
        for at in chunks(width):
            rows = pl.ds(at, CHUNK)
            for slot, field in zip(slots, works):
                wave = right_inverse((field[0, rows, :], field[1, rows, :]), turn, first)
                waves[slot, 0, rows, :] = wave[0]
                waves[slot, 1, rows, :] = wave[1]
        return carry

    lax.fori_loop(0, (count[0, 0] + 1) // 2, visit, 0)


def second_kernel(
    count, positions, tiles, side_a, side_b, strip_a, strip_b, waves, targets,
    turns, matrices,
    backs, centre, send_a, send_b, ext, acc, patch, work,
):
    width = waves.shape[2]
    half = width // 2
    assemble(ext, device_bits(), tiles.at[1], (side_a, side_b), (strip_a, strip_b))
    acc[...] = jnp.zeros_like(acc)

    first, second = matrices.at[0:2], matrices.at[2:4]

    def visit(pair_at, carry):
        pair = pair_of(count[0, 0], pair_at)
        slots = [slot for slot, weight in pair]
        places = [place(positions, slot, half) for slot in slots]
        works = [work.at[at] for at in range(2)]
        turn = lane_pair(turns)

        def misfit(slot, lanes, parity, value):
            rows = pl.ds(parity * half, half)
            level = value[0] * value[0] + value[1] * value[1] - targets[slot, rows, lanes]
            return level * value[0], level * value[1]

        for at in chunks(width):
            rows = pl.ds(at, CHUNK)
            for which, (slot, (row, base, shift)) in enumerate(zip(slots, places)):
                cells = tuple(
                    read_patch(ext, part, row + at, CHUNK, base, shift, half) for part in range(2)
                )
                for part in range(2):
                    patch[which, part, rows, :] = cells[part]
                exited = mul((waves[slot, 0, rows, :], waves[slot, 1, rows, :]), cells)
                out = right_forward(exited, turn, second)
                works[which][0, rows, :] = out[0]
                works[which][1, rows, :] = out[1]
        left_stage(works, turns, first, second, [functools.partial(misfit, slot) for slot in slots])
        for at in chunks(width):
            rows = pl.ds(at, CHUNK)
            for which, ((slot, weight), (row, base, shift)) in enumerate(zip(pair, places)):
                field = works[which]
                adjoint = right_inverse((field[0, rows, :], field[1, rows, :]), turn, first)
                wave = (waves[slot, 0, rows, :], waves[slot, 1, rows, :])
                term = conj_mul(wave, adjoint)
                for part in range(2):
                    add_patch(acc, part, row + at, base, shift, term[part] * weight)
                back = conj_mul((patch[which, 0, rows, :], patch[which, 1, rows, :]), adjoint)
                out = right_forward(back, turn, second)
                backs[slot, 0, rows, :] = out[0]
                backs[slot, 1, rows, :] = out[1]
        return carry

    lax.fori_loop(0, (count[0, 0] + 1) // 2, visit, 0)
    write_out(acc, device_bits(), centre, (send_a, send_b))


def third_kernel(
    count, positions, used, patches, backs, probe, transfer,
    turns, matrices,
    adjoints, keep, send, work, probe_sum,
):
    width = probe.shape[1]
    half = width // 2
    probe_sum[...] = jnp.zeros_like(probe_sum)

    def through(lanes, parity, value):
        rows = pl.ds(parity * half, half)
        return conj_mul((transfer[0, rows, lanes], transfer[1, rows, lanes]), value)

    first, second = matrices.at[0:2], matrices.at[2:4]

    def visit(pair_at, carry):
        pair = pair_of(count[0, 0], pair_at)
        turn = lane_pair(turns)
        works = [work.at[at] for at in range(2)]
        for (slot, weight), own in zip(pair, works):
            own[...] = backs[slot]
        left_stage(works, turns, first, second, [through] * 2)
        for at in chunks(width):
            rows = pl.ds(at, CHUNK)
            for field, (slot, weight) in zip(works, pair):
                adjoint = right_inverse((field[0, rows, :], field[1, rows, :]), turn, first)
                cells = (patches[slot, 0, rows, :], patches[slot, 1, rows, :])
                back = conj_mul(cells, adjoint)
                for part in range(2):
                    adjoints[slot, part, rows, :] = adjoint[part]
                    probe_sum[part, rows, :] = probe_sum[part, rows, :] + back[part] * weight
        return carry

    lax.fori_loop(0, (count[0, 0] + 1) // 2, visit, 0)
    mine = device_bits()[0]
    keep[:width, :] = probe_sum[mine]
    send[:width, :] = probe_sum[1 - mine]
    scalars = jnp.where(
        lax.broadcasted_iota(jnp.int32, (SCALARS, width), 0) < SCALARS // 2,
        jnp.full((SCALARS, width), used[0, 0], F32),
        jnp.full((SCALARS, width), count[0, 0].astype(F32), F32),
    )
    keep[width:, :] = scalars
    send[width:, :] = scalars


def fourth_kernel(count, positions, probe, adjoints, centre, send_a, send_b, acc):
    width = probe.shape[1]
    half = width // 2
    acc[...] = jnp.zeros_like(acc)

    def visit(slot_at, carry):
        row, base, shift = place(positions, slot_at, half)
        for at in chunks(width):
            rows = pl.ds(at, CHUNK)
            adjoint = (adjoints[slot_at, 0, rows, :], adjoints[slot_at, 1, rows, :])
            term = conj_mul((probe[0, rows, :], probe[1, rows, :]), adjoint)
            for part in range(2):
                add_patch(acc, part, row + at, base, shift, term[part])
        return carry

    lax.fori_loop(0, count[0, 0], visit, 0)
    write_out(acc, device_bits(), centre, (send_a, send_b))


def edges_kernel(tiles, *outs):
    bits = device_bits()
    half = outs[0].shape[2]
    for at in range(tiles.shape[0]):
        for out, start in zip(outs[2 * at : 2 * at + 2], other_end(bits[1], tiles.shape[3] - half)):
            out[...] = tiles[at, :, :, pl.ds(pl.multiple_of(start, half), half)]


def widen_kernel(at, tiles, side_a, side_b, strip_a, strip_b):
    bits = device_bits()
    half = side_a.shape[2]
    size = tiles.shape[3]
    sides = other_end(bits[1], half + size)
    for out, start in zip((strip_a, strip_b), other_end(bits[0], size - half)):
        rows = pl.ds(start, half)
        out[:, :, half : half + size] = tiles[at, :, rows, :]
        for side, lane in zip((side_a, side_b), sides):
            out[:, :, pl.ds(pl.multiple_of(lane, half), half)] = side[:, rows, :]


def by_parity(bit, work):
    @pl.when(bit == 0)
    def _():
        work(1, 0)

    @pl.when(bit == 1)
    def _():
        work(0, 1)


def rows_kernel(centre, strip_a, strip_b, owned, side_a, side_b):
    bits = device_bits()
    half = strip_a.shape[1]
    size = centre.shape[1]
    strips, sides = (strip_a, strip_b), (side_a, side_b)

    def add(above, below):
        def part_sides(before, after):
            for out, lanes in (
                (sides[before], slice(0, half)),
                (owned, slice(half, half + size)),
                (sides[after], slice(half + size, 2 * half + size)),
            ):
                out[:, :half, :] = centre[:, :half, lanes] + strips[above][:, :, lanes]
                if size > 2 * half:
                    out[:, half : size - half, :] = centre[:, half : size - half, lanes]
                out[:, size - half :, :] = centre[:, size - half :, lanes] + strips[below][:, :, lanes]

        by_parity(bits[1], part_sides)

    by_parity(bits[0], add)


def mean_factor(scalars, width):
    scans = scalars[SCALARS // 2 : SCALARS // 2 + 1, :]
    return scans * float(width * width) / scalars[0:1, :], scans


def finish_object_kernel(scalars, *refs):
    *sources, object_grad = refs
    factor, scans = mean_factor(scalars, scalars.shape[1])
    lanes = object_grad.shape[3]

    def add(before, after):
        for at in range(object_grad.shape[0]):
            owned = sources[3 * at]
            sides = sources[3 * at + 1 : 3 * at + 3]
            half = sides[0].shape[2]
            scale = factor[:, :half][None]
            object_grad[at, :, :, :half] = (owned[:, :, :half] + sides[before][...]) * scale
            for start in range(half, lanes - half, half):
                object_grad[at, :, :, start : start + half] = owned[:, :, start : start + half] * scale
            object_grad[at, :, :, lanes - half :] = (
                owned[:, :, lanes - half :] + sides[after][...]
            ) * scale

    by_parity(device_bits()[1], add)


def finish_probe_kernel(scalars, own, other, probe_grad):
    factor, scans = mean_factor(scalars, scalars.shape[1])
    factor = factor / scans
    core = device_bits()[0]
    probe_grad[core] = own[...] * factor
    probe_grad[1 - core] = other[...] * factor


def add_kernel(*refs):
    *terms, out = refs
    total = terms[0][...]
    for term in terms[1:]:
        total = total + term[...]
    out[...] = total


def halve_kernel(which, kept, received, keep, send):
    bits = device_bits()
    rows = keep.shape[0] - SCALARS

    def part(first, second):
        for out, start in ((keep, first * rows), (send, second * rows)):
            out[:rows, :] = kept[start : start + rows, :] + received[start : start + rows, :]
            out[rows:, :] = kept[2 * rows :, :] + received[2 * rows :, :]

    by_parity(1 - bits[which], part)


def join_kernel(*refs):
    bits = device_bits()
    *pieces, out = refs
    rows = pieces[0].shape[0]
    for at, piece in enumerate(pieces):
        spot = (bits[2] ^ (at >> 1)) * 2 + (bits[3] ^ (at & 1))
        out[pl.ds(pl.multiple_of(spot * rows, rows), rows), :] = piece[...]


SCALARS = 8

SMEM = pl.BlockSpec(memory_space=pltpu.SMEM)
VMEM = pl.BlockSpec(memory_space=pltpu.VMEM)


def call(kernel, outs, scratch, scalars, arrays, cost, name, out_specs=None):
    moved = sum(4 * array.size for array in arrays)
    limit = (20 if scratch else 10) * 1024 * 1024
    return pl.pallas_call(
        kernel,
        out_shape=[jax.ShapeDtypeStruct(shape, F32) for shape in outs],
        in_specs=[SMEM] * len(scalars) + [VMEM] * len(arrays),
        out_specs=out_specs or [VMEM] * len(outs),
        scratch_shapes=[pltpu.VMEM(shape, F32) for shape in scratch],
        compiler_params=pltpu.CompilerParams(vmem_limit_bytes=limit),
        cost_estimate=pl.CostEstimate(flops=cost * 10**9, bytes_accessed=moved, transcendentals=0),
        name=name,
    )(*scalars, *arrays)


def swap(value, axis, bit):
    return lax.ppermute(value, axis, [(i, i ^ bit) for i in range(lax.axis_size(axis))])


def swap_next(value, axis):
    odd = range(1, lax.axis_size(axis) - 1, 2)
    return lax.ppermute(value, axis, [pair for i in odd for pair in ((i, i + 1), (i + 1, i))])


def both_swaps(values, axis):
    return [swap(values[0], axis, 1), swap_next(values[1], axis)]


def higher_bits(axis, bit):
    while bit < lax.axis_size(axis):
        yield bit
        bit *= 2


def on_device(object_slices, probe, propagator, measured, positions, scan_counts):
    layers = object_slices.shape[0]
    tile = object_slices.shape[2]
    width = probe.shape[1]
    half = width // 2
    slots = measured.shape[2]
    long = 2 * half + tile
    matrices, turns = (jnp.asarray(value) for value in tables(width))
    transforms = [turns, matrices]
    fields = (slots, 2, width, width)
    side, strip, middle = (2, tile, half), (2, half, long), (2, tile, long)
    wide, one = (2, 3 + tile // half, long, half), (2, width, width)
    two = (2, *one)
    places = positions[0, 0].T

    edges = call(edges_kernel, [side] * (2 * layers), [], [], [object_slices], 0, "tile_edges")
    sides = [both_swaps(edges[2 * at : 2 * at + 2], "col") for at in range(layers)]
    targets, transfer, used = call(
        prepare_kernel, [(slots, width, width), one, (1, 1)], [], [scan_counts],
        [measured[0, 0], propagator, matrices],
        6, "reorder_targets", [VMEM, VMEM, SMEM],
    )
    sides[0], targets, transfer = lax.optimization_barrier((sides[0], targets, transfer))
    strips = []
    for at in range(layers):
        pair = call(
            functools.partial(widen_kernel, at), [strip, strip], [], [],
            [object_slices, *sides[at]], 20, "widen",
        )
        strips.append(both_swaps(pair, "row"))

    waves, patches = call(
        first_kernel, [fields, fields], [wide, two], [scan_counts, places],
        [object_slices, *sides[0], *strips[0], probe, transfer, *transforms], 20, "first_slice",
    )
    backs, centre, *ends = call(
        second_kernel, [fields, middle, strip, strip], [wide, wide, two, two], [scan_counts, places],
        [object_slices, *sides[1], *strips[1], waves, targets, *transforms], 20, "second_slice",
    )

    def add_rows(centre, ends, cost=20):
        return call(
            rows_kernel, [(2, tile, tile), side, side], [], [], [centre, *ends], cost, "add_rows"
        )

    def halve(which, kept, received, cost=0):
        half_shape = ((kept.shape[0] - SCALARS) // 2 + SCALARS, width)
        return call(
            functools.partial(halve_kernel, which), [half_shape, half_shape], [], [],
            [kept, received], cost, "halve",
        )

    ends_last, centre_last = both_swaps(ends, "row"), centre
    message = (width + SCALARS, width)
    adjoints, keep, send = call(
        third_kernel, [fields, message, message], [two, one], [scan_counts, places, used],
        [patches, backs, probe, transfer, *transforms], 20, "first_adjoint",
    )
    keep, send = halve(2, keep, swap(send, "row", 1))
    send, ends_last = lax.optimization_barrier((send, ends_last))
    owned_last, *sides_last = add_rows(centre_last, ends_last)
    sides_last = both_swaps(sides_last, "col")
    keep, send = halve(3, keep, swap(send, "row", 2), 20)
    send, adjoints = lax.optimization_barrier((send, adjoints))
    centre, *ends = call(
        fourth_kernel, [middle, strip, strip], [wide], [scan_counts, places],
        [probe, adjoints], 20, "first_gradient",
    )
    ends = both_swaps(ends, "row")
    (state,) = call(
        add_kernel, [keep.shape], [], [], [keep, swap(send, "row", 4)], 20, "add",
    )
    ends, sides_last = lax.optimization_barrier((ends, sides_last))
    owned_first, *sides_first = add_rows(centre, ends)
    sides_first = both_swaps(sides_first, "col")
    (state,) = call(add_kernel, [state.shape], [], [], [state, swap(state, "col", 1)], 20, "add")
    (state,) = call(add_kernel, [state.shape], [], [], [state, swap(state, "col", 2)], 0, "add")
    for axis, bit in (("col", 4), ("row", 8)):
        for bit in higher_bits(axis, bit):
            state = state + swap(state, axis, bit)
    scalars, mine = state[-SCALARS:], state[:-SCALARS]
    (own,) = call(
        join_kernel, [(width, width)], [], [],
        [mine, *(swap(mine, "row", bit) for bit in (4, 2, 6))], 0, "join",
    )
    other = swap(own, "row", 1)
    (object_grad,) = call(
        finish_object_kernel, [object_slices.shape], [], [],
        [scalars, owned_first, *sides_first, owned_last, *sides_last], 20, "finish_object",
    )
    other, object_grad = lax.optimization_barrier((other, object_grad))
    (probe_grad,) = call(finish_probe_kernel, [one], [], [], [scalars, own, other], 0, "finish_probe")
    return object_grad, probe_grad


def solution(mesh):
    placed = (
        P(None, None, "row", "col"),
        P(),
        P(),
        P("row", "col", None, None, None),
        P("row", "col", None, None),
        P("row", "col"),
    )
    return jax.shard_map(
        on_device,
        mesh=mesh,
        in_specs=placed,
        out_specs=(P(None, None, "row", "col"), P()),
        check_vma=False,
    )
```

```python
import functools

import jax
import jax.numpy as jnp
import numpy as np
from jax import lax
from jax.experimental import pallas as pl
from jax.experimental.pallas import tpu as pltpu
from jax.sharding import PartitionSpec as P

F32 = jnp.float32
BF16 = jnp.bfloat16


def split_table(table):
    high = table.astype(BF16)
    low = (table - high.astype(np.float64)).astype(BF16)
    return high, low


@functools.lru_cache(None)
def tables(width):
    half = width // 2
    index = np.arange(half)
    angle = 2.0 * np.pi * ((index[:, None] * index[None, :]) % half) / half
    cosine, sine = np.cos(angle) / np.sqrt(width), np.sin(angle) / np.sqrt(width)
    first = split_table(np.block([[cosine, sine], [-sine, cosine]]))
    second = split_table(np.block([[cosine, -sine], [sine, cosine]]))
    turn = 2.0 * np.pi * index / width
    turns = np.stack([np.cos(turn), np.sin(turn)]).astype(np.float32)
    row = np.broadcast_to(turns[:, :, None], (2, half, half))
    lane = np.broadcast_to(turns[:, None, :], (2, 8, half))
    spread = np.zeros((width, width))
    spread[np.arange(width), index_order(width)] = 1.0
    matrices = [*first, *second, spread.astype(BF16), spread.T.astype(BF16)]
    return np.stack(matrices), np.concatenate([row, lane], axis=1)


def index_order(width):
    index = np.arange(width)
    return index // 2 + (index % 2) * (width // 2)


def split(value):
    high = value.astype(BF16)
    low = (value - high.astype(F32)).astype(BF16)
    return high, low


def right_dot(value, matrix):
    high, low = split(value)
    return jnp.dot(
        jnp.concatenate([high, low, high], axis=1),
        jnp.concatenate([matrix[0], matrix[0], matrix[1]], axis=0),
        preferred_element_type=F32,
    )


def left_dot(matrix, value):
    high, low = split(value)
    return jnp.dot(
        jnp.concatenate([matrix[0], matrix[0], matrix[1]], axis=1),
        jnp.concatenate([high, low, high], axis=0),
        preferred_element_type=F32,
    )


def mul(a, b):
    return a[0] * b[0] - a[1] * b[1], a[0] * b[1] + a[1] * b[0]


def conj_mul(a, b):
    return a[0] * b[0] + a[1] * b[1], a[0] * b[1] - a[1] * b[0]


def right_forward(field, lane, matrix):
    half = field[0].shape[1] // 2
    rows = field[0].shape[0]
    a = tuple(part[:, :half] for part in field)
    b = tuple(part[:, half:] for part in field)
    u = (a[0] + b[0], a[1] + b[1])
    v = conj_mul(lane, (a[0] - b[0], a[1] - b[1]))
    stacked = jnp.concatenate(
        [jnp.concatenate(u, axis=1), jnp.concatenate(v, axis=1)], axis=0
    )
    out = right_dot(stacked, matrix)
    even, odd = out[:rows], out[rows:]
    return (
        jnp.concatenate([even[:, :half], odd[:, :half]], axis=1),
        jnp.concatenate([even[:, half:], odd[:, half:]], axis=1),
    )


def right_inverse(field, lane, matrix):
    half = field[0].shape[1] // 2
    rows = field[0].shape[0]
    even = jnp.concatenate([field[0][:, :half], field[1][:, :half]], axis=1)
    odd = jnp.concatenate([field[0][:, half:], field[1][:, half:]], axis=1)
    out = right_dot(jnp.concatenate([even, odd], axis=0), matrix)
    even, odd = out[:rows], out[rows:]
    even = (even[:, :half], even[:, half:])
    odd = mul(lane, (odd[:, :half], odd[:, half:]))
    return tuple(
        jnp.concatenate([e + o, e - o], axis=1) for e, o in zip(even, odd)
    )


def left_pair(field, row, forward, inverse, middle):
    half = field[0].shape[0] // 2
    lanes = field[0].shape[1]
    a = tuple(part[:half] for part in field)
    b = tuple(part[half:] for part in field)
    u = (a[0] + b[0], a[1] + b[1])
    v = conj_mul(row, (a[0] - b[0], a[1] - b[1]))
    stacked = jnp.concatenate(
        [jnp.concatenate(u, axis=0), jnp.concatenate(v, axis=0)], axis=1
    )
    out = left_dot(forward, stacked)
    even = middle(0, (out[:half, :lanes], out[half:, :lanes]))
    odd = middle(1, (out[:half, lanes:], out[half:, lanes:]))
    stacked = jnp.concatenate(
        [jnp.concatenate(even, axis=0), jnp.concatenate(odd, axis=0)], axis=1
    )
    out = left_dot(inverse, stacked)
    even = (out[:half, :lanes], out[half:, :lanes])
    odd = mul(row, (out[:half, lanes:], out[half:, lanes:]))
    return tuple(
        jnp.concatenate([e + o, e - o], axis=0) for e, o in zip(even, odd)
    )


def lane_pair(turns):
    half = turns.shape[2]
    return turns[0, half : half + 1, :], turns[1, half : half + 1, :]


def left_stage(works, turns, forward, inverse, middles):
    half = turns.shape[2]
    for at in range(works[0].shape[2] // half):
        lanes = pl.ds(at * half, half)
        for work, middle in zip(works, middles):
            out = left_pair(
                (work[0, :, lanes], work[1, :, lanes]),
                (turns[0, :half, :], turns[1, :half, :]),
                forward,
                inverse,
                functools.partial(middle, lanes),
            )
            work[0, :, lanes] = out[0]
            work[1, :, lanes] = out[1]


def pair_of(count, at):
    both = 2 * at + 1 < count
    second = 2 * at + both.astype(jnp.int32)
    return (2 * at, 1.0), (second, both.astype(F32))


def device_bits():
    row, col = lax.axis_index("row"), lax.axis_index("col")
    return row & 1, col & 1, (row >> 1) & 1, (row >> 2) & 1


def other_end(parity, span):
    return pl.multiple_of((1 - parity) * span, 8), pl.multiple_of(parity * span, 8)


def assemble(ext, bits, tile, sides, strips):
    half = sides[0].shape[2]
    size = tile.shape[1]
    blocks = size // half
    for part in range(2):
        for at in range(blocks):
            ext[part, 1 + at, half : half + size, :] = tile[part, :, at * half : (at + 1) * half]
        for side, at in zip(sides, ((1 - bits[1]) * (blocks + 1), bits[1] * (blocks + 1))):
            ext[part, at, half : half + size, :] = side[part]
        for strip, start in zip(strips, other_end(bits[0], half + size)):
            for at in range(blocks + 2):
                ext[part, at, pl.ds(start, half), :] = strip[part, :, at * half : (at + 1) * half]


def place(places, slot_at, half):
    row = places[0, slot_at] + half
    col = places[1, slot_at] + half
    return row, col // half, col % half


def read_patch(ext, part, row, rows, base, shift, half):
    blocks = []
    for at in range(3):
        block = ext[part, base + at, pl.ds(row, rows), :]
        blocks.append(pltpu.roll(block, lax.rem(half - shift, half), 1))
    own = lax.broadcasted_iota(jnp.int32, (rows, half), 1) < half - shift
    return jnp.concatenate(
        [jnp.where(own, blocks[0], blocks[1]), jnp.where(own, blocks[1], blocks[2])], axis=1
    )


def add_patch(acc, part, row, base, shift, value):
    rows, width = value.shape
    half = width // 2
    first = pltpu.roll(value[:, :half], shift, 1)
    second = pltpu.roll(value[:, half:], shift, 1)
    own = lax.broadcasted_iota(jnp.int32, (rows, half), 1) >= shift
    zero = jnp.zeros_like(first)
    blocks = (
        jnp.where(own, first, zero),
        jnp.where(own, second, first),
        jnp.where(own, zero, second),
    )
    for at, block in enumerate(blocks):
        spot = (part, base + at, pl.ds(row, rows), slice(None))
        acc[spot] = acc[spot] + block


def write_out(acc, bits, centre, strips):
    half = acc.shape[3]
    size = centre.shape[1]
    for part in range(2):
        for at in range(centre.shape[2] // half):
            lanes = slice(at * half, (at + 1) * half)
            centre[part, :, lanes] = acc[part, at, half : half + size, :]
            for strip, start in zip(strips, other_end(bits[0], half + size)):
                strip[part, :, lanes] = acc[part, at, pl.ds(start, half), :]


CHUNK = 128


def chunks(width):
    return range(0, width, CHUNK)


def three_parts(value):
    high = value.astype(BF16)
    rest = value - high.astype(F32)
    middle = rest.astype(BF16)
    return high, middle, (rest - middle.astype(F32)).astype(BF16)


def prepare_kernel(places, measured, propagator, matrices, targets, kernel_out, level_scalars):
    slots = measured.shape[0]

    def reorder(source, at, out):
        moved = jnp.dot(
            jnp.concatenate(three_parts(source[at]), axis=1),
            jnp.concatenate([matrices[4]] * 3, axis=0),
            preferred_element_type=F32,
        )
        out[at] = jnp.dot(
            jnp.concatenate([matrices[5]] * 3, axis=1),
            jnp.concatenate(three_parts(moved), axis=0),
            preferred_element_type=F32,
        )

    used = jnp.float32(0.0)
    for slot_at in range(slots):
        reorder(measured, slot_at, targets)
        sums = jnp.sum(measured[slot_at])
        used = used + jnp.where(slot_at < places[2, 0], sums, jnp.float32(0.0))
    for part in range(2):
        reorder(propagator, part, kernel_out)
    width = level_scalars.shape[1]
    level_scalars[...] = jnp.where(
        lax.broadcasted_iota(jnp.int32, (SCALARS, width), 0) < SCALARS // 2,
        jnp.full((SCALARS, width), used, F32),
        jnp.full((SCALARS, width), places[2, 0].astype(F32), F32),
    )


def first_kernel(
    places, tiles, side_a, side_b, strip_a, strip_b, probe, transfer,
    turns, matrices,
    waves, patches, ext, work,
):
    width = probe.shape[1]
    half = width // 2
    assemble(ext, device_bits(), tiles.at[0], (side_a, side_b), (strip_a, strip_b))

    def through(lanes, parity, value):
        rows = pl.ds(parity * half, half)
        return mul((transfer[0, rows, lanes], transfer[1, rows, lanes]), value)

    first, second = matrices.at[0:2], matrices.at[2:4]

    def visit(pair_at, carry):
        slots = [slot for slot, weight in pair_of(places[2, 0], pair_at)]
        spots = [place(places, slot, half) for slot in slots]
        works = [work.at[at] for at in range(2)]
        turn = lane_pair(turns)
        for at in chunks(width):
            rows = pl.ds(at, CHUNK)
            for slot, (row, base, shift), field in zip(slots, spots, works):
                patch = tuple(
                    read_patch(ext, part, row + at, CHUNK, base, shift, half) for part in range(2)
                )
                for part in range(2):
                    patches[slot, part, rows, :] = patch[part]
                exited = mul((probe[0, rows, :], probe[1, rows, :]), patch)
                out = right_forward(exited, turn, second)
                field[0, rows, :] = out[0]
                field[1, rows, :] = out[1]
        left_stage(works, turns, first, second, [through] * 2)
        for at in chunks(width):
            rows = pl.ds(at, CHUNK)
            for slot, field in zip(slots, works):
                wave = right_inverse((field[0, rows, :], field[1, rows, :]), turn, first)
                waves[slot, 0, rows, :] = wave[0]
                waves[slot, 1, rows, :] = wave[1]
        return carry

    lax.fori_loop(0, (places[2, 0] + 1) // 2, visit, 0)


def second_kernel(
    places, tiles, side_a, side_b, strip_a, strip_b, waves, targets,
    turns, matrices,
    backs, centre, send_a, send_b, ext, acc, patch, work,
):
    width = waves.shape[2]
    half = width // 2
    assemble(ext, device_bits(), tiles.at[1], (side_a, side_b), (strip_a, strip_b))
    acc[...] = jnp.zeros_like(acc)

    first, second = matrices.at[0:2], matrices.at[2:4]

    def visit(pair_at, carry):
        pair = pair_of(places[2, 0], pair_at)
        slots = [slot for slot, weight in pair]
        spots = [place(places, slot, half) for slot in slots]
        works = [work.at[at] for at in range(2)]
        turn = lane_pair(turns)

        def misfit(slot, lanes, parity, value):
            rows = pl.ds(parity * half, half)
            level = value[0] * value[0] + value[1] * value[1] - targets[slot, rows, lanes]
            return level * value[0], level * value[1]

        for at in chunks(width):
            rows = pl.ds(at, CHUNK)
            for which, (slot, (row, base, shift)) in enumerate(zip(slots, spots)):
                cells = tuple(
                    read_patch(ext, part, row + at, CHUNK, base, shift, half) for part in range(2)
                )
                for part in range(2):
                    patch[which, part, rows, :] = cells[part]
                exited = mul((waves[slot, 0, rows, :], waves[slot, 1, rows, :]), cells)
                out = right_forward(exited, turn, second)
                works[which][0, rows, :] = out[0]
                works[which][1, rows, :] = out[1]
        left_stage(works, turns, first, second, [functools.partial(misfit, slot) for slot in slots])
        for at in chunks(width):
            rows = pl.ds(at, CHUNK)
            for which, ((slot, weight), (row, base, shift)) in enumerate(zip(pair, spots)):
                field = works[which]
                adjoint = right_inverse((field[0, rows, :], field[1, rows, :]), turn, first)
                wave = (waves[slot, 0, rows, :], waves[slot, 1, rows, :])
                term = conj_mul(wave, adjoint)
                for part in range(2):
                    add_patch(acc, part, row + at, base, shift, term[part] * weight)
                back = conj_mul((patch[which, 0, rows, :], patch[which, 1, rows, :]), adjoint)
                out = right_forward(back, turn, second)
                backs[slot, 0, rows, :] = out[0]
                backs[slot, 1, rows, :] = out[1]
        return carry

    lax.fori_loop(0, (places[2, 0] + 1) // 2, visit, 0)
    write_out(acc, device_bits(), centre, (send_a, send_b))


def third_kernel(
    places, level_scalars, patches, backs, probe, transfer,
    turns, matrices,
    adjoints, keep, send, work, probe_sum,
):
    width = probe.shape[1]
    half = width // 2
    probe_sum[...] = jnp.zeros_like(probe_sum)

    def through(lanes, parity, value):
        rows = pl.ds(parity * half, half)
        return conj_mul((transfer[0, rows, lanes], transfer[1, rows, lanes]), value)

    first, second = matrices.at[0:2], matrices.at[2:4]

    def visit(pair_at, carry):
        pair = pair_of(places[2, 0], pair_at)
        turn = lane_pair(turns)
        works = [work.at[at] for at in range(2)]
        for (slot, weight), own in zip(pair, works):
            own[...] = backs[slot]
        left_stage(works, turns, first, second, [through] * 2)
        for at in chunks(width):
            rows = pl.ds(at, CHUNK)
            for field, (slot, weight) in zip(works, pair):
                adjoint = right_inverse((field[0, rows, :], field[1, rows, :]), turn, first)
                cells = (patches[slot, 0, rows, :], patches[slot, 1, rows, :])
                back = conj_mul(cells, adjoint)
                for part in range(2):
                    adjoints[slot, part, rows, :] = adjoint[part]
                    probe_sum[part, rows, :] = probe_sum[part, rows, :] + back[part] * weight
        return carry

    lax.fori_loop(0, (places[2, 0] + 1) // 2, visit, 0)
    mine = device_bits()[0]
    keep[:width, :] = probe_sum[mine]
    send[:width, :] = probe_sum[1 - mine]
    scalars = level_scalars[...]
    keep[width:, :] = scalars
    send[width:, :] = scalars


def fourth_kernel(places, probe, adjoints, centre, send_a, send_b, acc):
    width = probe.shape[1]
    half = width // 2
    acc[...] = jnp.zeros_like(acc)

    def visit(slot_at, carry):
        row, base, shift = place(places, slot_at, half)
        for at in chunks(width):
            rows = pl.ds(at, CHUNK)
            adjoint = (adjoints[slot_at, 0, rows, :], adjoints[slot_at, 1, rows, :])
            term = conj_mul((probe[0, rows, :], probe[1, rows, :]), adjoint)
            for part in range(2):
                add_patch(acc, part, row + at, base, shift, term[part])
        return carry

    lax.fori_loop(0, places[2, 0], visit, 0)
    write_out(acc, device_bits(), centre, (send_a, send_b))


def edges_kernel(tiles, *outs):
    bits = device_bits()
    half = outs[0].shape[2]
    for at in range(tiles.shape[0]):
        for out, start in zip(outs[2 * at : 2 * at + 2], other_end(bits[1], tiles.shape[3] - half)):
            out[...] = tiles[at, :, :, pl.ds(pl.multiple_of(start, half), half)]


def widen_kernel(at, tiles, side_a, side_b, strip_a, strip_b):
    bits = device_bits()
    half = side_a.shape[2]
    size = tiles.shape[3]
    sides = other_end(bits[1], half + size)
    for out, start in zip((strip_a, strip_b), other_end(bits[0], size - half)):
        rows = pl.ds(start, half)
        out[:, :, half : half + size] = tiles[at, :, rows, :]
        for side, lane in zip((side_a, side_b), sides):
            out[:, :, pl.ds(pl.multiple_of(lane, half), half)] = side[:, rows, :]


def by_parity(bit, work):
    @pl.when(bit == 0)
    def _():
        work(1, 0)

    @pl.when(bit == 1)
    def _():
        work(0, 1)


def rows_kernel(centre, strip_a, strip_b, owned, side_a, side_b):
    bits = device_bits()
    half = strip_a.shape[1]
    size = centre.shape[1]
    strips, sides = (strip_a, strip_b), (side_a, side_b)

    def add(above, below):
        def part_sides(before, after):
            for out, lanes in (
                (sides[before], slice(0, half)),
                (owned, slice(half, half + size)),
                (sides[after], slice(half + size, 2 * half + size)),
            ):
                out[:, :half, :] = centre[:, :half, lanes] + strips[above][:, :, lanes]
                if size > 2 * half:
                    out[:, half : size - half, :] = centre[:, half : size - half, lanes]
                out[:, size - half :, :] = centre[:, size - half :, lanes] + strips[below][:, :, lanes]

        by_parity(bits[1], part_sides)

    by_parity(bits[0], add)


def mean_factor(scalars, width):
    scans = scalars[SCALARS // 2 : SCALARS // 2 + 1, :]
    return scans * float(width * width) / scalars[0:1, :], scans


def finish_object_kernel(scalars, *refs):
    *sources, object_grad = refs
    factor, scans = mean_factor(scalars, scalars.shape[1])
    lanes = object_grad.shape[3]

    def add(before, after):
        for at in range(object_grad.shape[0]):
            owned = sources[3 * at]
            sides = sources[3 * at + 1 : 3 * at + 3]
            half = sides[0].shape[2]
            scale = factor[:, :half][None]
            object_grad[at, :, :, :half] = (owned[:, :, :half] + sides[before][...]) * scale
            for start in range(half, lanes - half, half):
                object_grad[at, :, :, start : start + half] = owned[:, :, start : start + half] * scale
            object_grad[at, :, :, lanes - half :] = (
                owned[:, :, lanes - half :] + sides[after][...]
            ) * scale

    by_parity(device_bits()[1], add)


def finish_probe_kernel(scalars, own, other, probe_grad):
    factor, scans = mean_factor(scalars, scalars.shape[1])
    factor = factor / scans
    core = device_bits()[0]
    probe_grad[core] = own[...] * factor
    probe_grad[1 - core] = other[...] * factor


def add_kernel(*refs):
    *terms, out = refs
    total = terms[0][...]
    for term in terms[1:]:
        total = total + term[...]
    out[...] = total


def halve_kernel(which, kept, received, keep, send):
    bits = device_bits()
    rows = keep.shape[0] - SCALARS

    def part(first, second):
        for out, start in ((keep, first * rows), (send, second * rows)):
            out[:rows, :] = kept[start : start + rows, :] + received[start : start + rows, :]
            out[rows:, :] = kept[2 * rows :, :] + received[2 * rows :, :]

    by_parity(1 - bits[which], part)


def join_kernel(*refs):
    bits = device_bits()
    *pieces, out = refs
    rows = pieces[0].shape[0]
    for at, piece in enumerate(pieces):
        spot = (bits[2] ^ (at >> 1)) * 2 + (bits[3] ^ (at & 1))
        out[pl.ds(pl.multiple_of(spot * rows, rows), rows), :] = piece[...]


SCALARS = 8

SMEM = pl.BlockSpec(memory_space=pltpu.SMEM)
VMEM = pl.BlockSpec(memory_space=pltpu.VMEM)


def call(kernel, outs, scratch, scalars, arrays, cost, name, out_specs=None):
    moved = sum(4 * array.size for array in arrays)
    limit = (20 if scratch else 10) * 1024 * 1024
    return pl.pallas_call(
        kernel,
        out_shape=[jax.ShapeDtypeStruct(shape, F32) for shape in outs],
        in_specs=[SMEM] * len(scalars) + [VMEM] * len(arrays),
        out_specs=out_specs or [VMEM] * len(outs),
        scratch_shapes=[pltpu.VMEM(shape, F32) for shape in scratch],
        compiler_params=pltpu.CompilerParams(vmem_limit_bytes=limit),
        cost_estimate=pl.CostEstimate(flops=cost * 10**9, bytes_accessed=moved, transcendentals=0),
        name=name,
    )(*scalars, *arrays)


def swap(value, axis, bit):
    return lax.ppermute(value, axis, [(i, i ^ bit) for i in range(lax.axis_size(axis))])


def swap_next(value, axis):
    odd = range(1, lax.axis_size(axis) - 1, 2)
    return lax.ppermute(value, axis, [pair for i in odd for pair in ((i, i + 1), (i + 1, i))])


def both_swaps(values, axis):
    return [swap(values[0], axis, 1), swap_next(values[1], axis)]


def higher_bits(axis, bit):
    while bit < lax.axis_size(axis):
        yield bit
        bit *= 2


def on_device(object_slices, probe, propagator, measured, positions, scan_counts):
    layers = object_slices.shape[0]
    tile = object_slices.shape[2]
    width = probe.shape[1]
    half = width // 2
    slots = measured.shape[2]
    long = 2 * half + tile
    matrices, turns = (jnp.asarray(value) for value in tables(width))
    transforms = [turns, matrices]
    fields = (slots, 2, width, width)
    side, strip, middle = (2, tile, half), (2, half, long), (2, tile, long)
    wide, one = (2, 3 + tile // half, long, half), (2, width, width)
    two = (2, *one)
    places = jnp.concatenate([positions[0, 0].T, jnp.broadcast_to(scan_counts, (1, slots))], axis=0)

    edges = call(edges_kernel, [side] * (2 * layers), [], [], [object_slices], 0, "tile_edges")
    sides = [both_swaps(edges[2 * at : 2 * at + 2], "col") for at in range(layers)]
    targets, transfer, level_scalars = call(
        prepare_kernel, [(slots, width, width), one, (SCALARS, width)], [], [places],
        [measured[0, 0], propagator, matrices],
        6, "reorder_targets",
    )
    sides[0], targets, transfer = lax.optimization_barrier((sides[0], targets, transfer))
    strips = []
    for at in range(layers):
        pair = call(
            functools.partial(widen_kernel, at), [strip, strip], [], [],
            [object_slices, *sides[at]], 20, "widen",
        )
        strips.append(both_swaps(pair, "row"))

    waves, patches = call(
        first_kernel, [fields, fields], [wide, two], [places],
        [object_slices, *sides[0], *strips[0], probe, transfer, *transforms], 20, "first_slice",
    )
    backs, centre, *ends = call(
        second_kernel, [fields, middle, strip, strip], [wide, wide, two, two], [places],
        [object_slices, *sides[1], *strips[1], waves, targets, *transforms], 20, "second_slice",
    )

    def add_rows(centre, ends, cost=20):
        return call(
            rows_kernel, [(2, tile, tile), side, side], [], [], [centre, *ends], cost, "add_rows"
        )

    def halve(which, kept, received, cost=0):
        half_shape = ((kept.shape[0] - SCALARS) // 2 + SCALARS, width)
        return call(
            functools.partial(halve_kernel, which), [half_shape, half_shape], [], [],
            [kept, received], cost, "halve",
        )

    ends_last, centre_last = both_swaps(ends, "row"), centre
    message = (width + SCALARS, width)
    adjoints, keep, send = call(
        third_kernel, [fields, message, message], [two, one], [places],
        [level_scalars, patches, backs, probe, transfer, *transforms], 20, "first_adjoint",
    )
    centre, *ends = call(
        fourth_kernel, [middle, strip, strip], [wide], [places],
        [probe, adjoints], 0, "first_gradient",
    )
    received, centre, ends = lax.optimization_barrier((swap(send, "row", 1), centre, ends))
    keep, send = halve(2, keep, received)
    send, ends, ends_last = lax.optimization_barrier((send, ends, ends_last))
    ends = both_swaps(ends, "row")
    owned_last, *sides_last = add_rows(centre_last, ends_last)
    sides_last = both_swaps(sides_last, "col")
    keep, send = halve(3, keep, swap(send, "row", 2), 20)
    state = keep + swap(send, "row", 4)
    state, ends, sides_last = lax.optimization_barrier((state, ends, sides_last))
    owned_first, *sides_first = add_rows(centre, ends)
    sides_first = both_swaps(sides_first, "col")
    (state,) = call(
        add_kernel, [state.shape], [], [],
        [state, *(swap(state, "col", bit) for bit in range(1, 4))], 20, "add",
    )
    for axis, bit in (("col", 4), ("row", 8)):
        for bit in higher_bits(axis, bit):
            state = state + swap(state, axis, bit)
    scalars, mine = state[-SCALARS:], state[:-SCALARS]
    (own,) = call(
        join_kernel, [(width, width)], [], [],
        [mine, *(swap(mine, "row", bit) for bit in (4, 2, 6))], 0, "join",
    )
    other = swap(own, "row", 1)
    (object_grad,) = call(
        finish_object_kernel, [object_slices.shape], [], [],
        [scalars, owned_first, *sides_first, owned_last, *sides_last], 20, "finish_object",
    )
    other, object_grad = lax.optimization_barrier((other, object_grad))
    (probe_grad,) = call(finish_probe_kernel, [one], [], [], [scalars, own, other], 0, "finish_probe")
    return object_grad, probe_grad


def solution(mesh):
    placed = (
        P(None, None, "row", "col"),
        P(),
        P(),
        P("row", "col", None, None, None),
        P("row", "col", None, None),
        P("row", "col"),
    )
    return jax.shard_map(
        on_device,
        mesh=mesh,
        in_specs=placed,
        out_specs=(P(None, None, "row", "col"), P()),
        check_vma=False,
    )
```

```python
import functools

import jax
import jax.numpy as jnp
import numpy as np
from jax import lax
from jax.experimental import pallas as pl
from jax.experimental.pallas import tpu as pltpu
from jax.sharding import PartitionSpec as P

F32 = jnp.float32
BF16 = jnp.bfloat16


def split_table(table):
    high = table.astype(BF16)
    low = (table - high.astype(np.float64)).astype(BF16)
    return high, low


@functools.lru_cache(None)
def tables(width):
    half = width // 2
    index = np.arange(half)
    angle = 2.0 * np.pi * ((index[:, None] * index[None, :]) % half) / half
    cosine, sine = np.cos(angle) / np.sqrt(width), np.sin(angle) / np.sqrt(width)
    first = split_table(np.block([[cosine, sine], [-sine, cosine]]))
    second = split_table(np.block([[cosine, -sine], [sine, cosine]]))
    turn = 2.0 * np.pi * index / width
    turns = np.stack([np.cos(turn), np.sin(turn)]).astype(np.float32)
    row = np.broadcast_to(turns[:, :, None], (2, half, half))
    lane = np.broadcast_to(turns[:, None, :], (2, 8, half))
    spread = np.zeros((width, width))
    spread[np.arange(width), index_order(width)] = 1.0
    matrices = [*first, *second, spread.astype(BF16), spread.T.astype(BF16)]
    return np.stack(matrices), np.concatenate([row, lane], axis=1)


def index_order(width):
    index = np.arange(width)
    return index // 2 + (index % 2) * (width // 2)


def split(value):
    high = value.astype(BF16)
    low = (value - high.astype(F32)).astype(BF16)
    return high, low


def right_dot(value, matrix):
    high, low = split(value)
    return jnp.dot(
        jnp.concatenate([high, low, high], axis=1),
        jnp.concatenate([matrix[0], matrix[0], matrix[1]], axis=0),
        preferred_element_type=F32,
    )


def left_dot(matrix, value):
    high, low = split(value)
    return jnp.dot(
        jnp.concatenate([matrix[0], matrix[0], matrix[1]], axis=1),
        jnp.concatenate([high, low, high], axis=0),
        preferred_element_type=F32,
    )


def mul(a, b):
    return a[0] * b[0] - a[1] * b[1], a[0] * b[1] + a[1] * b[0]


def conj_mul(a, b):
    return a[0] * b[0] + a[1] * b[1], a[0] * b[1] - a[1] * b[0]


def right_forward(field, lane, matrix):
    half = field[0].shape[1] // 2
    rows = field[0].shape[0]
    a = tuple(part[:, :half] for part in field)
    b = tuple(part[:, half:] for part in field)
    u = (a[0] + b[0], a[1] + b[1])
    v = conj_mul(lane, (a[0] - b[0], a[1] - b[1]))
    stacked = jnp.concatenate(
        [jnp.concatenate(u, axis=1), jnp.concatenate(v, axis=1)], axis=0
    )
    out = right_dot(stacked, matrix)
    even, odd = out[:rows], out[rows:]
    return (
        jnp.concatenate([even[:, :half], odd[:, :half]], axis=1),
        jnp.concatenate([even[:, half:], odd[:, half:]], axis=1),
    )


def right_inverse(field, lane, matrix):
    half = field[0].shape[1] // 2
    rows = field[0].shape[0]
    even = jnp.concatenate([field[0][:, :half], field[1][:, :half]], axis=1)
    odd = jnp.concatenate([field[0][:, half:], field[1][:, half:]], axis=1)
    out = right_dot(jnp.concatenate([even, odd], axis=0), matrix)
    even, odd = out[:rows], out[rows:]
    even = (even[:, :half], even[:, half:])
    odd = mul(lane, (odd[:, :half], odd[:, half:]))
    return tuple(
        jnp.concatenate([e + o, e - o], axis=1) for e, o in zip(even, odd)
    )


def left_pair(field, row, forward, inverse, middle):
    half = field[0].shape[0] // 2
    lanes = field[0].shape[1]
    a = tuple(part[:half] for part in field)
    b = tuple(part[half:] for part in field)
    u = (a[0] + b[0], a[1] + b[1])
    v = conj_mul(row, (a[0] - b[0], a[1] - b[1]))
    stacked = jnp.concatenate(
        [jnp.concatenate(u, axis=0), jnp.concatenate(v, axis=0)], axis=1
    )
    out = left_dot(forward, stacked)
    even = middle(0, (out[:half, :lanes], out[half:, :lanes]))
    odd = middle(1, (out[:half, lanes:], out[half:, lanes:]))
    stacked = jnp.concatenate(
        [jnp.concatenate(even, axis=0), jnp.concatenate(odd, axis=0)], axis=1
    )
    out = left_dot(inverse, stacked)
    even = (out[:half, :lanes], out[half:, :lanes])
    odd = mul(row, (out[:half, lanes:], out[half:, lanes:]))
    return tuple(
        jnp.concatenate([e + o, e - o], axis=0) for e, o in zip(even, odd)
    )


def lane_pair(turns):
    half = turns.shape[2]
    return turns[0, half : half + 1, :], turns[1, half : half + 1, :]


def left_stage(works, turns, forward, inverse, middles):
    half = turns.shape[2]
    for at in range(works[0].shape[2] // half):
        lanes = pl.ds(at * half, half)
        for work, middle in zip(works, middles):
            out = left_pair(
                (work[0, :, lanes], work[1, :, lanes]),
                (turns[0, :half, :], turns[1, :half, :]),
                forward,
                inverse,
                functools.partial(middle, lanes),
            )
            work[0, :, lanes] = out[0]
            work[1, :, lanes] = out[1]


def pair_of(count, at):
    both = 2 * at + 1 < count
    second = 2 * at + both.astype(jnp.int32)
    return (2 * at, 1.0), (second, both.astype(F32))


def device_bits():
    row, col = lax.axis_index("row"), lax.axis_index("col")
    return row & 1, col & 1, (row >> 1) & 1, (row >> 2) & 1


def other_end(parity, span):
    return pl.multiple_of((1 - parity) * span, 8), pl.multiple_of(parity * span, 8)


def assemble(ext, bits, tile, sides, strips):
    half = sides[0].shape[2]
    size = tile.shape[1]
    blocks = size // half
    for part in range(2):
        for at in range(blocks):
            ext[part, 1 + at, half : half + size, :] = tile[part, :, at * half : (at + 1) * half]
        for side, at in zip(sides, ((1 - bits[1]) * (blocks + 1), bits[1] * (blocks + 1))):
            ext[part, at, half : half + size, :] = side[part]
        for strip, start in zip(strips, other_end(bits[0], half + size)):
            for at in range(blocks + 2):
                ext[part, at, pl.ds(start, half), :] = strip[part, :, at * half : (at + 1) * half]


def place(places, slot_at, half):
    row = places[0, slot_at] + half
    col = places[1, slot_at] + half
    return row, col // half, col % half


def read_patch(ext, part, row, rows, base, shift, half):
    blocks = []
    for at in range(3):
        block = ext[part, base + at, pl.ds(row, rows), :]
        blocks.append(pltpu.roll(block, lax.rem(half - shift, half), 1))
    own = lax.broadcasted_iota(jnp.int32, (rows, half), 1) < half - shift
    return jnp.concatenate(
        [jnp.where(own, blocks[0], blocks[1]), jnp.where(own, blocks[1], blocks[2])], axis=1
    )


def add_patch(acc, part, row, base, shift, value):
    rows, width = value.shape
    half = width // 2
    first = pltpu.roll(value[:, :half], shift, 1)
    second = pltpu.roll(value[:, half:], shift, 1)
    own = lax.broadcasted_iota(jnp.int32, (rows, half), 1) >= shift
    zero = jnp.zeros_like(first)
    blocks = (
        jnp.where(own, first, zero),
        jnp.where(own, second, first),
        jnp.where(own, zero, second),
    )
    for at, block in enumerate(blocks):
        spot = (part, base + at, pl.ds(row, rows), slice(None))
        acc[spot] = acc[spot] + block


def write_out(acc, bits, centre, strips):
    half = acc.shape[3]
    size = centre.shape[1]
    for part in range(2):
        for at in range(centre.shape[2] // half):
            lanes = slice(at * half, (at + 1) * half)
            centre[part, :, lanes] = acc[part, at, half : half + size, :]
            for strip, start in zip(strips, other_end(bits[0], half + size)):
                strip[part, :, lanes] = acc[part, at, pl.ds(start, half), :]


CHUNK = 128


def chunks(width):
    return range(0, width, CHUNK)


def three_parts(value):
    high = value.astype(BF16)
    rest = value - high.astype(F32)
    middle = rest.astype(BF16)
    return high, middle, (rest - middle.astype(F32)).astype(BF16)


def prepare_kernel(places, measured, propagator, matrices, targets, kernel_out, level_scalars):
    slots = measured.shape[0]

    def reorder(source, at, out):
        moved = jnp.dot(
            jnp.concatenate(three_parts(source[at]), axis=1),
            jnp.concatenate([matrices[4]] * 3, axis=0),
            preferred_element_type=F32,
        )
        out[at] = jnp.dot(
            jnp.concatenate([matrices[5]] * 3, axis=1),
            jnp.concatenate(three_parts(moved), axis=0),
            preferred_element_type=F32,
        )

    used = jnp.float32(0.0)
    for slot_at in range(slots):
        reorder(measured, slot_at, targets)
        sums = jnp.sum(measured[slot_at])
        used = used + jnp.where(slot_at < places[2, 0], sums, jnp.float32(0.0))
    for part in range(2):
        reorder(propagator, part, kernel_out)
    width = level_scalars.shape[1]
    level_scalars[...] = jnp.where(
        lax.broadcasted_iota(jnp.int32, (SCALARS, width), 0) < SCALARS // 2,
        jnp.full((SCALARS, width), used, F32),
        jnp.full((SCALARS, width), places[2, 0].astype(F32), F32),
    )


def first_kernel(
    places, tiles, side_a, side_b, strip_b, strip_a, probe, transfer,
    turns, matrices,
    waves, patches, ext, work,
):
    width = probe.shape[1]
    half = width // 2
    assemble(ext, device_bits(), tiles.at[0], (side_a, side_b), (strip_a, strip_b))

    def through(lanes, parity, value):
        rows = pl.ds(parity * half, half)
        return mul((transfer[0, rows, lanes], transfer[1, rows, lanes]), value)

    first, second = matrices.at[0:2], matrices.at[2:4]

    def visit(pair_at, carry):
        slots = [slot for slot, weight in pair_of(places[2, 0], pair_at)]
        spots = [place(places, slot, half) for slot in slots]
        works = [work.at[at] for at in range(2)]
        turn = lane_pair(turns)
        for at in chunks(width):
            rows = pl.ds(at, CHUNK)
            for slot, (row, base, shift), field in zip(slots, spots, works):
                patch = tuple(
                    read_patch(ext, part, row + at, CHUNK, base, shift, half) for part in range(2)
                )
                for part in range(2):
                    patches[slot, part, rows, :] = patch[part]
                exited = mul((probe[0, rows, :], probe[1, rows, :]), patch)
                out = right_forward(exited, turn, second)
                field[0, rows, :] = out[0]
                field[1, rows, :] = out[1]
        left_stage(works, turns, first, second, [through] * 2)
        for at in chunks(width):
            rows = pl.ds(at, CHUNK)
            for slot, field in zip(slots, works):
                wave = right_inverse((field[0, rows, :], field[1, rows, :]), turn, first)
                waves[slot, 0, rows, :] = wave[0]
                waves[slot, 1, rows, :] = wave[1]
        return carry

    lax.fori_loop(0, (places[2, 0] + 1) // 2, visit, 0)


def second_kernel(
    places, tiles, side_a, side_b, strip_b, strip_a, waves, targets,
    turns, matrices,
    backs, centre, send_a, send_b, ext, acc, patch, work,
):
    width = waves.shape[2]
    half = width // 2
    assemble(ext, device_bits(), tiles.at[1], (side_a, side_b), (strip_a, strip_b))
    acc[...] = jnp.zeros_like(acc)

    first, second = matrices.at[0:2], matrices.at[2:4]

    def visit(pair_at, carry):
        pair = pair_of(places[2, 0], pair_at)
        slots = [slot for slot, weight in pair]
        spots = [place(places, slot, half) for slot in slots]
        works = [work.at[at] for at in range(2)]
        turn = lane_pair(turns)

        def misfit(slot, lanes, parity, value):
            rows = pl.ds(parity * half, half)
            level = value[0] * value[0] + value[1] * value[1] - targets[slot, rows, lanes]
            return level * value[0], level * value[1]

        for at in chunks(width):
            rows = pl.ds(at, CHUNK)
            for which, (slot, (row, base, shift)) in enumerate(zip(slots, spots)):
                cells = tuple(
                    read_patch(ext, part, row + at, CHUNK, base, shift, half) for part in range(2)
                )
                for part in range(2):
                    patch[which, part, rows, :] = cells[part]
                exited = mul((waves[slot, 0, rows, :], waves[slot, 1, rows, :]), cells)
                out = right_forward(exited, turn, second)
                works[which][0, rows, :] = out[0]
                works[which][1, rows, :] = out[1]
        left_stage(works, turns, first, second, [functools.partial(misfit, slot) for slot in slots])
        for at in chunks(width):
            rows = pl.ds(at, CHUNK)
            for which, ((slot, weight), (row, base, shift)) in enumerate(zip(pair, spots)):
                field = works[which]
                adjoint = right_inverse((field[0, rows, :], field[1, rows, :]), turn, first)
                wave = (waves[slot, 0, rows, :], waves[slot, 1, rows, :])
                term = conj_mul(wave, adjoint)
                for part in range(2):
                    add_patch(acc, part, row + at, base, shift, term[part] * weight)
                back = conj_mul((patch[which, 0, rows, :], patch[which, 1, rows, :]), adjoint)
                out = right_forward(back, turn, second)
                backs[slot, 0, rows, :] = out[0]
                backs[slot, 1, rows, :] = out[1]
        return carry

    lax.fori_loop(0, (places[2, 0] + 1) // 2, visit, 0)
    write_out(acc, device_bits(), centre, (send_a, send_b))


def third_kernel(
    places, level_scalars, patches, backs, probe, transfer,
    turns, matrices,
    adjoints, keep, send, work, probe_sum,
):
    width = probe.shape[1]
    half = width // 2
    probe_sum[...] = jnp.zeros_like(probe_sum)

    def through(lanes, parity, value):
        rows = pl.ds(parity * half, half)
        return conj_mul((transfer[0, rows, lanes], transfer[1, rows, lanes]), value)

    first, second = matrices.at[0:2], matrices.at[2:4]

    def visit(pair_at, carry):
        pair = pair_of(places[2, 0], pair_at)
        turn = lane_pair(turns)
        works = [work.at[at] for at in range(2)]
        for (slot, weight), own in zip(pair, works):
            own[...] = backs[slot]
        left_stage(works, turns, first, second, [through] * 2)
        for at in chunks(width):
            rows = pl.ds(at, CHUNK)
            for field, (slot, weight) in zip(works, pair):
                adjoint = right_inverse((field[0, rows, :], field[1, rows, :]), turn, first)
                cells = (patches[slot, 0, rows, :], patches[slot, 1, rows, :])
                back = conj_mul(cells, adjoint)
                for part in range(2):
                    adjoints[slot, part, rows, :] = adjoint[part]
                    probe_sum[part, rows, :] = probe_sum[part, rows, :] + back[part] * weight
        return carry

    lax.fori_loop(0, (places[2, 0] + 1) // 2, visit, 0)
    mine = device_bits()[0]
    keep[:width, :] = probe_sum[mine]
    send[:width, :] = probe_sum[1 - mine]
    scalars = level_scalars[...]
    keep[width:, :] = scalars
    send[width:, :] = scalars


def fourth_kernel(places, probe, adjoints, centre, send_a, send_b, acc):
    width = probe.shape[1]
    half = width // 2
    acc[...] = jnp.zeros_like(acc)

    def visit(slot_at, carry):
        row, base, shift = place(places, slot_at, half)
        for at in chunks(width):
            rows = pl.ds(at, CHUNK)
            adjoint = (adjoints[slot_at, 0, rows, :], adjoints[slot_at, 1, rows, :])
            term = conj_mul((probe[0, rows, :], probe[1, rows, :]), adjoint)
            for part in range(2):
                add_patch(acc, part, row + at, base, shift, term[part])
        return carry

    lax.fori_loop(0, places[2, 0], visit, 0)
    write_out(acc, device_bits(), centre, (send_a, send_b))


def edges_kernel(tiles, *outs):
    bits = device_bits()
    half = outs[0].shape[2]
    for at in range(tiles.shape[0]):
        for out, start in zip(outs[2 * at : 2 * at + 2], other_end(bits[1], tiles.shape[3] - half)):
            out[...] = tiles[at, :, :, pl.ds(pl.multiple_of(start, half), half)]


def widen_kernel(at, tiles, side_a, side_b, strip_a, strip_b):
    bits = device_bits()
    half = side_a.shape[2]
    size = tiles.shape[3]
    sides = other_end(bits[1], half + size)
    for out, start in zip((strip_a, strip_b), other_end(bits[0], size - half)):
        rows = pl.ds(start, half)
        out[:, :, half : half + size] = tiles[at, :, rows, :]
        for side, lane in zip((side_a, side_b), sides):
            out[:, :, pl.ds(pl.multiple_of(lane, half), half)] = side[:, rows, :]


def by_parity(bit, work):
    @pl.when(bit == 0)
    def _():
        work(1, 0)

    @pl.when(bit == 1)
    def _():
        work(0, 1)


def rows_kernel(centre, strip_b, strip_a, owned, side_a, side_b):
    bits = device_bits()
    half = strip_a.shape[1]
    size = centre.shape[1]
    strips, sides = (strip_a, strip_b), (side_a, side_b)

    def add(above, below):
        def part_sides(before, after):
            for out, lanes in (
                (sides[before], slice(0, half)),
                (owned, slice(half, half + size)),
                (sides[after], slice(half + size, 2 * half + size)),
            ):
                out[:, :half, :] = centre[:, :half, lanes] + strips[above][:, :, lanes]
                if size > 2 * half:
                    out[:, half : size - half, :] = centre[:, half : size - half, lanes]
                out[:, size - half :, :] = centre[:, size - half :, lanes] + strips[below][:, :, lanes]

        by_parity(bits[1], part_sides)

    by_parity(bits[0], add)


def mean_factor(scalars, width):
    scans = scalars[SCALARS // 2 : SCALARS // 2 + 1, :]
    return scans * float(width * width) / scalars[0:1, :], scans


def finish_object_kernel(scalars, *refs):
    *sources, object_grad = refs
    factor, scans = mean_factor(scalars, scalars.shape[1])
    lanes = object_grad.shape[3]

    def add(before, after):
        for at in range(object_grad.shape[0]):
            owned = sources[3 * at]
            sides = sources[3 * at + 1 : 3 * at + 3]
            half = sides[0].shape[2]
            scale = factor[:, :half][None]
            object_grad[at, :, :, :half] = (owned[:, :, :half] + sides[before][...]) * scale
            for start in range(half, lanes - half, half):
                object_grad[at, :, :, start : start + half] = owned[:, :, start : start + half] * scale
            object_grad[at, :, :, lanes - half :] = (
                owned[:, :, lanes - half :] + sides[after][...]
            ) * scale

    by_parity(device_bits()[1], add)


def finish_probe_kernel(scalars, own, other, probe_grad):
    factor, scans = mean_factor(scalars, scalars.shape[1])
    factor = factor / scans
    core = device_bits()[0]
    probe_grad[core] = own[...] * factor
    probe_grad[1 - core] = other[...] * factor


def add_kernel(*refs):
    *terms, out = refs
    total = terms[0][...]
    for term in terms[1:]:
        total = total + term[...]
    out[...] = total


def halve_kernel(which, kept, received, keep, send):
    bits = device_bits()
    rows = keep.shape[0] - SCALARS

    def part(first, second):
        for out, start in ((keep, first * rows), (send, second * rows)):
            out[:rows, :] = kept[start : start + rows, :] + received[start : start + rows, :]
            out[rows:, :] = kept[2 * rows :, :] + received[2 * rows :, :]

    by_parity(1 - bits[which], part)


def join_kernel(*refs):
    bits = device_bits()
    *pieces, out = refs
    rows = pieces[0].shape[0]
    for at, piece in enumerate(pieces):
        spot = (bits[2] ^ (at >> 1)) * 2 + (bits[3] ^ (at & 1))
        out[pl.ds(pl.multiple_of(spot * rows, rows), rows), :] = piece[...]


SCALARS = 8

SMEM = pl.BlockSpec(memory_space=pltpu.SMEM)
VMEM = pl.BlockSpec(memory_space=pltpu.VMEM)


def call(kernel, outs, scratch, scalars, arrays, cost, name, out_specs=None):
    moved = sum(4 * array.size for array in arrays)
    limit = (20 if scratch else 10) * 1024 * 1024
    return pl.pallas_call(
        kernel,
        out_shape=[jax.ShapeDtypeStruct(shape, F32) for shape in outs],
        in_specs=[SMEM] * len(scalars) + [VMEM] * len(arrays),
        out_specs=out_specs or [VMEM] * len(outs),
        scratch_shapes=[pltpu.VMEM(shape, F32) for shape in scratch],
        compiler_params=pltpu.CompilerParams(vmem_limit_bytes=limit),
        cost_estimate=pl.CostEstimate(flops=cost * 10**9, bytes_accessed=moved, transcendentals=0),
        name=name,
    )(*scalars, *arrays)


def swap(value, axis, bit):
    return lax.ppermute(value, axis, [(i, i ^ bit) for i in range(lax.axis_size(axis))])


def swap_next(value, axis):
    odd = range(1, lax.axis_size(axis) - 1, 2)
    return lax.ppermute(value, axis, [pair for i in odd for pair in ((i, i + 1), (i + 1, i))])


def both_swaps(values, axis):
    if axis == "row":
        later = swap_next(values[1], axis)
        return [later, swap(values[0], axis, 1)]
    return [swap(values[0], axis, 1), swap_next(values[1], axis)]


def higher_bits(axis, bit):
    while bit < lax.axis_size(axis):
        yield bit
        bit *= 2


def on_device(object_slices, probe, propagator, measured, positions, scan_counts):
    layers = object_slices.shape[0]
    tile = object_slices.shape[2]
    width = probe.shape[1]
    half = width // 2
    slots = measured.shape[2]
    long = 2 * half + tile
    matrices, turns = (jnp.asarray(value) for value in tables(width))
    transforms = [turns, matrices]
    fields = (slots, 2, width, width)
    side, strip, middle = (2, tile, half), (2, half, long), (2, tile, long)
    wide, one = (2, 3 + tile // half, long, half), (2, width, width)
    two = (2, *one)
    places = jnp.concatenate([positions[0, 0].T, jnp.broadcast_to(scan_counts, (1, slots))], axis=0)

    edges = call(edges_kernel, [side] * (2 * layers), [], [], [object_slices], 0, "tile_edges")
    sides = [both_swaps(edges[2 * at : 2 * at + 2], "col") for at in range(layers)]
    targets, transfer, level_scalars = call(
        prepare_kernel, [(slots, width, width), one, (SCALARS, width)], [], [places],
        [measured[0, 0], propagator, matrices],
        6, "reorder_targets",
    )
    sides[0], targets, transfer = lax.optimization_barrier((sides[0], targets, transfer))
    strips = []
    for at in range(layers):
        pair = call(
            functools.partial(widen_kernel, at), [strip, strip], [], [],
            [object_slices, *sides[at]], 20, "widen",
        )
        strips.append(both_swaps(pair, "row"))

    waves, patches = call(
        first_kernel, [fields, fields], [wide, two], [places],
        [object_slices, *sides[0], *strips[0], probe, transfer, *transforms], 20, "first_slice",
    )
    backs, centre, *ends = call(
        second_kernel, [fields, middle, strip, strip], [wide, wide, two, two], [places],
        [object_slices, *sides[1], *strips[1], waves, targets, *transforms], 20, "second_slice",
    )

    def add_rows(centre, ends, cost=20):
        return call(
            rows_kernel, [(2, tile, tile), side, side], [], [], [centre, *ends], cost, "add_rows"
        )

    def halve(which, kept, received, cost=0):
        half_shape = ((kept.shape[0] - SCALARS) // 2 + SCALARS, width)
        return call(
            functools.partial(halve_kernel, which), [half_shape, half_shape], [], [],
            [kept, received], cost, "halve",
        )

    ends_last, centre_last = both_swaps(ends, "row"), centre
    message = (width + SCALARS, width)
    adjoints, keep, send = call(
        third_kernel, [fields, message, message], [two, one], [places],
        [level_scalars, patches, backs, probe, transfer, *transforms], 20, "first_adjoint",
    )
    centre, *ends = call(
        fourth_kernel, [middle, strip, strip], [wide], [places],
        [probe, adjoints], 0, "first_gradient",
    )
    received, centre, ends = lax.optimization_barrier((swap(send, "row", 1), centre, ends))
    keep, send = halve(2, keep, received)
    send, ends, ends_last = lax.optimization_barrier((send, ends, ends_last))
    ends = both_swaps(ends, "row")
    owned_last, *sides_last = add_rows(centre_last, ends_last)
    sides_last = both_swaps(sides_last, "col")
    keep, send = halve(3, keep, swap(send, "row", 2), 20)
    state = keep + swap(send, "row", 4)
    state, ends, sides_last = lax.optimization_barrier((state, ends, sides_last))
    owned_first, *sides_first = add_rows(centre, ends)
    sides_first = both_swaps(sides_first, "col")
    (state,) = call(
        add_kernel, [state.shape], [], [],
        [state, *(swap(state, "col", bit) for bit in range(1, 4))], 20, "add",
    )
    for axis, bit in (("col", 4), ("row", 8)):
        for bit in higher_bits(axis, bit):
            state = state + swap(state, axis, bit)
    scalars, mine = state[-SCALARS:], state[:-SCALARS]
    (own,) = call(
        join_kernel, [(width, width)], [], [],
        [mine, *(swap(mine, "row", bit) for bit in (4, 2, 6))], 0, "join",
    )
    other = swap(own, "row", 1)
    (object_grad,) = call(
        finish_object_kernel, [object_slices.shape], [], [],
        [scalars, owned_first, *sides_first, owned_last, *sides_last], 20, "finish_object",
    )
    other, object_grad = lax.optimization_barrier((other, object_grad))
    (probe_grad,) = call(finish_probe_kernel, [one], [], [], [scalars, own, other], 0, "finish_probe")
    return object_grad, probe_grad


def solution(mesh):
    placed = (
        P(None, None, "row", "col"),
        P(),
        P(),
        P("row", "col", None, None, None),
        P("row", "col", None, None),
        P("row", "col"),
    )
    return jax.shard_map(
        on_device,
        mesh=mesh,
        in_specs=placed,
        out_specs=(P(None, None, "row", "col"), P()),
        check_vma=False,
    )
```

```python
import functools

import jax
import jax.numpy as jnp
import numpy as np
from jax import lax
from jax.experimental import pallas as pl
from jax.experimental.pallas import tpu as pltpu
from jax.sharding import PartitionSpec as P

F32 = jnp.float32
BF16 = jnp.bfloat16


def split_table(table):
    high = table.astype(BF16)
    low = (table - high.astype(np.float64)).astype(BF16)
    return high, low


@functools.lru_cache(None)
def tables(width):
    half = width // 2
    index = np.arange(half)
    angle = 2.0 * np.pi * ((index[:, None] * index[None, :]) % half) / half
    cosine, sine = np.cos(angle) / np.sqrt(width), np.sin(angle) / np.sqrt(width)
    first = split_table(np.block([[cosine, sine], [-sine, cosine]]))
    second = split_table(np.block([[cosine, -sine], [sine, cosine]]))
    turn = 2.0 * np.pi * index / width
    turns = np.stack([np.cos(turn), np.sin(turn)]).astype(np.float32)
    row = np.broadcast_to(turns[:, :, None], (2, half, half))
    lane = np.broadcast_to(turns[:, None, :], (2, 8, half))
    spread = np.zeros((width, width))
    spread[np.arange(width), index_order(width)] = 1.0
    matrices = [*first, *second, spread.astype(BF16), spread.T.astype(BF16)]
    return np.stack(matrices), np.concatenate([row, lane], axis=1)


def index_order(width):
    index = np.arange(width)
    return index // 2 + (index % 2) * (width // 2)


def split(value):
    high = value.astype(BF16)
    low = (value - high.astype(F32)).astype(BF16)
    return high, low


def right_dot(value, matrix):
    high, low = split(value)
    rows = value.shape[0]
    both = jnp.dot(jnp.concatenate([high, low], axis=0), matrix[0], preferred_element_type=F32)
    rest = jnp.dot(high, matrix[1], preferred_element_type=F32)
    return both[:rows] + (both[rows:] + rest)


def left_dot(matrix, value):
    high, low = split(value)
    rows = matrix[0].shape[0]
    both = jnp.dot(
        jnp.concatenate([matrix[0], matrix[1]], axis=0), high, preferred_element_type=F32
    )
    rest = jnp.dot(matrix[0], low, preferred_element_type=F32)
    return both[:rows] + (both[rows:] + rest)


def mul(a, b):
    return a[0] * b[0] - a[1] * b[1], a[0] * b[1] + a[1] * b[0]


def conj_mul(a, b):
    return a[0] * b[0] + a[1] * b[1], a[0] * b[1] - a[1] * b[0]


def right_forward(field, lane, matrix):
    half = field[0].shape[1] // 2
    rows = field[0].shape[0]
    a = tuple(part[:, :half] for part in field)
    b = tuple(part[:, half:] for part in field)
    u = (a[0] + b[0], a[1] + b[1])
    v = conj_mul(lane, (a[0] - b[0], a[1] - b[1]))
    stacked = jnp.concatenate(
        [jnp.concatenate(u, axis=1), jnp.concatenate(v, axis=1)], axis=0
    )
    out = right_dot(stacked, matrix)
    even, odd = out[:rows], out[rows:]
    return (
        jnp.concatenate([even[:, :half], odd[:, :half]], axis=1),
        jnp.concatenate([even[:, half:], odd[:, half:]], axis=1),
    )


def right_inverse(field, lane, matrix):
    half = field[0].shape[1] // 2
    rows = field[0].shape[0]
    even = jnp.concatenate([field[0][:, :half], field[1][:, :half]], axis=1)
    odd = jnp.concatenate([field[0][:, half:], field[1][:, half:]], axis=1)
    out = right_dot(jnp.concatenate([even, odd], axis=0), matrix)
    even, odd = out[:rows], out[rows:]
    even = (even[:, :half], even[:, half:])
    odd = mul(lane, (odd[:, :half], odd[:, half:]))
    return tuple(
        jnp.concatenate([e + o, e - o], axis=1) for e, o in zip(even, odd)
    )


def left_pair(field, row, forward, inverse, middle):
    half = field[0].shape[0] // 2
    lanes = field[0].shape[1]
    a = tuple(part[:half] for part in field)
    b = tuple(part[half:] for part in field)
    u = (a[0] + b[0], a[1] + b[1])
    v = conj_mul(row, (a[0] - b[0], a[1] - b[1]))
    stacked = jnp.concatenate(
        [jnp.concatenate(u, axis=0), jnp.concatenate(v, axis=0)], axis=1
    )
    out = left_dot(forward, stacked)
    even = middle(0, (out[:half, :lanes], out[half:, :lanes]))
    odd = middle(1, (out[:half, lanes:], out[half:, lanes:]))
    stacked = jnp.concatenate(
        [jnp.concatenate(even, axis=0), jnp.concatenate(odd, axis=0)], axis=1
    )
    out = left_dot(inverse, stacked)
    even = (out[:half, :lanes], out[half:, :lanes])
    odd = mul(row, (out[:half, lanes:], out[half:, lanes:]))
    return tuple(
        jnp.concatenate([e + o, e - o], axis=0) for e, o in zip(even, odd)
    )


def lane_pair(turns):
    half = turns.shape[2]
    return turns[0, half : half + 1, :], turns[1, half : half + 1, :]


def left_stage(works, turns, forward, inverse, middles):
    half = turns.shape[2]
    for at in range(works[0].shape[2] // half):
        lanes = pl.ds(at * half, half)
        for work, middle in zip(works, middles):
            out = left_pair(
                (work[0, :, lanes], work[1, :, lanes]),
                (turns[0, :half, :], turns[1, :half, :]),
                forward,
                inverse,
                functools.partial(middle, lanes),
            )
            work[0, :, lanes] = out[0]
            work[1, :, lanes] = out[1]


def pair_of(count, at):
    both = 2 * at + 1 < count
    second = 2 * at + both.astype(jnp.int32)
    return (2 * at, 1.0), (second, both.astype(F32))


def device_bits():
    row, col = lax.axis_index("row"), lax.axis_index("col")
    return row & 1, col & 1, (row >> 1) & 1, (row >> 2) & 1


def other_end(parity, span):
    return pl.multiple_of((1 - parity) * span, 8), pl.multiple_of(parity * span, 8)


def assemble(ext, bits, tile, sides, strips):
    half = sides[0].shape[2]
    size = tile.shape[1]
    blocks = size // half
    for part in range(2):
        for at in range(blocks):
            ext[part, 1 + at, half : half + size, :] = tile[part, :, at * half : (at + 1) * half]
        for side, at in zip(sides, ((1 - bits[1]) * (blocks + 1), bits[1] * (blocks + 1))):
            ext[part, at, half : half + size, :] = side[part]
        for strip, start in zip(strips, other_end(bits[0], half + size)):
            for at in range(blocks + 2):
                ext[part, at, pl.ds(start, half), :] = strip[part, :, at * half : (at + 1) * half]


def place(places, slot_at, half):
    row = places[0, slot_at] + half
    col = places[1, slot_at] + half
    return row, col // half, col % half


def read_patch(ext, part, row, rows, base, shift, half):
    blocks = []
    for at in range(3):
        block = ext[part, base + at, pl.ds(row, rows), :]
        blocks.append(pltpu.roll(block, lax.rem(half - shift, half), 1))
    own = lax.broadcasted_iota(jnp.int32, (rows, half), 1) < half - shift
    return jnp.concatenate(
        [jnp.where(own, blocks[0], blocks[1]), jnp.where(own, blocks[1], blocks[2])], axis=1
    )


def add_patch(acc, part, row, base, shift, value):
    rows, width = value.shape
    half = width // 2
    first = pltpu.roll(value[:, :half], shift, 1)
    second = pltpu.roll(value[:, half:], shift, 1)
    own = lax.broadcasted_iota(jnp.int32, (rows, half), 1) >= shift
    zero = jnp.zeros_like(first)
    blocks = (
        jnp.where(own, first, zero),
        jnp.where(own, second, first),
        jnp.where(own, zero, second),
    )
    for at, block in enumerate(blocks):
        spot = (part, base + at, pl.ds(row, rows), slice(None))
        acc[spot] = acc[spot] + block


def write_out(acc, bits, centre, strips):
    half = acc.shape[3]
    size = centre.shape[1]
    for part in range(2):
        for at in range(centre.shape[2] // half):
            lanes = slice(at * half, (at + 1) * half)
            centre[part, :, lanes] = acc[part, at, half : half + size, :]
            for strip, start in zip(strips, other_end(bits[0], half + size)):
                strip[part, :, lanes] = acc[part, at, pl.ds(start, half), :]


CHUNK = 128


def chunks(width):
    return range(0, width, CHUNK)


def three_parts(value):
    high = value.astype(BF16)
    rest = value - high.astype(F32)
    middle = rest.astype(BF16)
    return high, middle, (rest - middle.astype(F32)).astype(BF16)


def prepare_kernel(places, measured, propagator, matrices, targets, kernel_out, level_scalars):
    slots = measured.shape[0]

    def reorder(source, at, out):
        moved = jnp.dot(
            jnp.concatenate(three_parts(source[at]), axis=1),
            jnp.concatenate([matrices[4]] * 3, axis=0),
            preferred_element_type=F32,
        )
        out[at] = jnp.dot(
            jnp.concatenate([matrices[5]] * 3, axis=1),
            jnp.concatenate(three_parts(moved), axis=0),
            preferred_element_type=F32,
        )

    used = jnp.float32(0.0)
    for slot_at in range(slots):
        reorder(measured, slot_at, targets)
        sums = jnp.sum(measured[slot_at])
        used = used + jnp.where(slot_at < places[2, 0], sums, jnp.float32(0.0))
    for part in range(2):
        reorder(propagator, part, kernel_out)
    width = level_scalars.shape[1]
    level_scalars[...] = jnp.where(
        lax.broadcasted_iota(jnp.int32, (SCALARS, width), 0) < SCALARS // 2,
        jnp.full((SCALARS, width), used, F32),
        jnp.full((SCALARS, width), places[2, 0].astype(F32), F32),
    )


def first_kernel(
    places, tiles, side_a, side_b, strip_b, strip_a, probe, transfer,
    turns, matrices,
    waves, patches, ext, work,
):
    width = probe.shape[1]
    half = width // 2
    assemble(ext, device_bits(), tiles.at[0], (side_a, side_b), (strip_a, strip_b))

    def through(lanes, parity, value):
        rows = pl.ds(parity * half, half)
        return mul((transfer[0, rows, lanes], transfer[1, rows, lanes]), value)

    first, second = matrices.at[0:2], matrices.at[2:4]

    def visit(pair_at, carry):
        slots = [slot for slot, weight in pair_of(places[2, 0], pair_at)]
        spots = [place(places, slot, half) for slot in slots]
        works = [work.at[at] for at in range(2)]
        turn = lane_pair(turns)
        for at in chunks(width):
            rows = pl.ds(at, CHUNK)
            for slot, (row, base, shift), field in zip(slots, spots, works):
                patch = tuple(
                    read_patch(ext, part, row + at, CHUNK, base, shift, half) for part in range(2)
                )
                for part in range(2):
                    patches[slot, part, rows, :] = patch[part]
                exited = mul((probe[0, rows, :], probe[1, rows, :]), patch)
                out = right_forward(exited, turn, second)
                field[0, rows, :] = out[0]
                field[1, rows, :] = out[1]
        left_stage(works, turns, first, second, [through] * 2)
        for at in chunks(width):
            rows = pl.ds(at, CHUNK)
            for slot, field in zip(slots, works):
                wave = right_inverse((field[0, rows, :], field[1, rows, :]), turn, first)
                waves[slot, 0, rows, :] = wave[0]
                waves[slot, 1, rows, :] = wave[1]
        return carry

    lax.fori_loop(0, (places[2, 0] + 1) // 2, visit, 0)


def second_kernel(
    places, tiles, side_a, side_b, strip_b, strip_a, waves, targets,
    turns, matrices,
    backs, centre, send_a, send_b, ext, acc, patch, work,
):
    width = waves.shape[2]
    half = width // 2
    assemble(ext, device_bits(), tiles.at[1], (side_a, side_b), (strip_a, strip_b))
    acc[...] = jnp.zeros_like(acc)

    first, second = matrices.at[0:2], matrices.at[2:4]

    def visit(pair_at, carry):
        pair = pair_of(places[2, 0], pair_at)
        slots = [slot for slot, weight in pair]
        spots = [place(places, slot, half) for slot in slots]
        works = [work.at[at] for at in range(2)]
        turn = lane_pair(turns)

        def misfit(slot, lanes, parity, value):
            rows = pl.ds(parity * half, half)
            level = value[0] * value[0] + value[1] * value[1] - targets[slot, rows, lanes]
            return level * value[0], level * value[1]

        for at in chunks(width):
            rows = pl.ds(at, CHUNK)
            for which, (slot, (row, base, shift)) in enumerate(zip(slots, spots)):
                cells = tuple(
                    read_patch(ext, part, row + at, CHUNK, base, shift, half) for part in range(2)
                )
                for part in range(2):
                    patch[which, part, rows, :] = cells[part]
                exited = mul((waves[slot, 0, rows, :], waves[slot, 1, rows, :]), cells)
                out = right_forward(exited, turn, second)
                works[which][0, rows, :] = out[0]
                works[which][1, rows, :] = out[1]
        left_stage(works, turns, first, second, [functools.partial(misfit, slot) for slot in slots])
        for at in chunks(width):
            rows = pl.ds(at, CHUNK)
            for which, ((slot, weight), (row, base, shift)) in enumerate(zip(pair, spots)):
                field = works[which]
                adjoint = right_inverse((field[0, rows, :], field[1, rows, :]), turn, first)
                wave = (waves[slot, 0, rows, :], waves[slot, 1, rows, :])
                term = conj_mul(wave, adjoint)
                for part in range(2):
                    add_patch(acc, part, row + at, base, shift, term[part] * weight)
                back = conj_mul((patch[which, 0, rows, :], patch[which, 1, rows, :]), adjoint)
                out = right_forward(back, turn, second)
                backs[slot, 0, rows, :] = out[0]
                backs[slot, 1, rows, :] = out[1]
        return carry

    lax.fori_loop(0, (places[2, 0] + 1) // 2, visit, 0)
    write_out(acc, device_bits(), centre, (send_a, send_b))


def third_kernel(
    places, level_scalars, patches, backs, probe, transfer,
    turns, matrices,
    adjoints, keep, send, work, probe_sum,
):
    width = probe.shape[1]
    half = width // 2
    probe_sum[...] = jnp.zeros_like(probe_sum)

    def through(lanes, parity, value):
        rows = pl.ds(parity * half, half)
        return conj_mul((transfer[0, rows, lanes], transfer[1, rows, lanes]), value)

    first, second = matrices.at[0:2], matrices.at[2:4]

    def visit(pair_at, carry):
        pair = pair_of(places[2, 0], pair_at)
        turn = lane_pair(turns)
        works = [work.at[at] for at in range(2)]
        for (slot, weight), own in zip(pair, works):
            own[...] = backs[slot]
        left_stage(works, turns, first, second, [through] * 2)
        for at in chunks(width):
            rows = pl.ds(at, CHUNK)
            for field, (slot, weight) in zip(works, pair):
                adjoint = right_inverse((field[0, rows, :], field[1, rows, :]), turn, first)
                cells = (patches[slot, 0, rows, :], patches[slot, 1, rows, :])
                back = conj_mul(cells, adjoint)
                for part in range(2):
                    adjoints[slot, part, rows, :] = adjoint[part]
                    probe_sum[part, rows, :] = probe_sum[part, rows, :] + back[part] * weight
        return carry

    lax.fori_loop(0, (places[2, 0] + 1) // 2, visit, 0)
    mine = device_bits()[0]
    keep[:width, :] = probe_sum[mine]
    send[:width, :] = probe_sum[1 - mine]
    scalars = level_scalars[...]
    keep[width:, :] = scalars
    send[width:, :] = scalars


def fourth_kernel(places, probe, adjoints, centre, send_a, send_b, acc):
    width = probe.shape[1]
    half = width // 2
    acc[...] = jnp.zeros_like(acc)

    def visit(slot_at, carry):
        row, base, shift = place(places, slot_at, half)
        for at in chunks(width):
            rows = pl.ds(at, CHUNK)
            adjoint = (adjoints[slot_at, 0, rows, :], adjoints[slot_at, 1, rows, :])
            term = conj_mul((probe[0, rows, :], probe[1, rows, :]), adjoint)
            for part in range(2):
                add_patch(acc, part, row + at, base, shift, term[part])
        return carry

    lax.fori_loop(0, places[2, 0], visit, 0)
    write_out(acc, device_bits(), centre, (send_a, send_b))


def edges_kernel(tiles, *outs):
    bits = device_bits()
    half = outs[0].shape[2]
    for at in range(tiles.shape[0]):
        for out, start in zip(outs[2 * at : 2 * at + 2], other_end(bits[1], tiles.shape[3] - half)):
            out[...] = tiles[at, :, :, pl.ds(pl.multiple_of(start, half), half)]


def widen_kernel(at, tiles, side_a, side_b, strip_a, strip_b):
    bits = device_bits()
    half = side_a.shape[2]
    size = tiles.shape[3]
    sides = other_end(bits[1], half + size)
    for out, start in zip((strip_a, strip_b), other_end(bits[0], size - half)):
        rows = pl.ds(start, half)
        out[:, :, half : half + size] = tiles[at, :, rows, :]
        for side, lane in zip((side_a, side_b), sides):
            out[:, :, pl.ds(pl.multiple_of(lane, half), half)] = side[:, rows, :]


def by_parity(bit, work):
    @pl.when(bit == 0)
    def _():
        work(1, 0)

    @pl.when(bit == 1)
    def _():
        work(0, 1)


def rows_kernel(centre, strip_b, strip_a, owned, side_a, side_b):
    bits = device_bits()
    half = strip_a.shape[1]
    size = centre.shape[1]
    strips, sides = (strip_a, strip_b), (side_a, side_b)

    def add(above, below):
        def part_sides(before, after):
            for out, lanes in (
                (sides[before], slice(0, half)),
                (owned, slice(half, half + size)),
                (sides[after], slice(half + size, 2 * half + size)),
            ):
                out[:, :half, :] = centre[:, :half, lanes] + strips[above][:, :, lanes]
                if size > 2 * half:
                    out[:, half : size - half, :] = centre[:, half : size - half, lanes]
                out[:, size - half :, :] = centre[:, size - half :, lanes] + strips[below][:, :, lanes]

        by_parity(bits[1], part_sides)

    by_parity(bits[0], add)


def mean_factor(scalars, width):
    scans = scalars[SCALARS // 2 : SCALARS // 2 + 1, :]
    return scans * float(width * width) / scalars[0:1, :], scans


def finish_object_kernel(scalars, *refs):
    *sources, object_grad = refs
    factor, scans = mean_factor(scalars, scalars.shape[1])
    lanes = object_grad.shape[3]

    def add(before, after):
        for at in range(object_grad.shape[0]):
            owned = sources[3 * at]
            sides = sources[3 * at + 1 : 3 * at + 3]
            half = sides[0].shape[2]
            scale = factor[:, :half][None]
            object_grad[at, :, :, :half] = (owned[:, :, :half] + sides[before][...]) * scale
            for start in range(half, lanes - half, half):
                object_grad[at, :, :, start : start + half] = owned[:, :, start : start + half] * scale
            object_grad[at, :, :, lanes - half :] = (
                owned[:, :, lanes - half :] + sides[after][...]
            ) * scale

    by_parity(device_bits()[1], add)


def finish_probe_kernel(scalars, own, other, probe_grad):
    factor, scans = mean_factor(scalars, scalars.shape[1])
    factor = factor / scans
    core = device_bits()[0]
    probe_grad[core] = own[...] * factor
    probe_grad[1 - core] = other[...] * factor


def add_kernel(*refs):
    *terms, out = refs
    total = terms[0][...]
    for term in terms[1:]:
        total = total + term[...]
    out[...] = total


def halve_kernel(which, kept, received, keep, send):
    bits = device_bits()
    rows = keep.shape[0] - SCALARS

    def part(first, second):
        for out, start in ((keep, first * rows), (send, second * rows)):
            out[:rows, :] = kept[start : start + rows, :] + received[start : start + rows, :]
            out[rows:, :] = kept[2 * rows :, :] + received[2 * rows :, :]

    by_parity(1 - bits[which], part)


def join_kernel(*refs):
    bits = device_bits()
    *pieces, out = refs
    rows = pieces[0].shape[0]
    for at, piece in enumerate(pieces):
        spot = (bits[2] ^ (at >> 1)) * 2 + (bits[3] ^ (at & 1))
        out[pl.ds(pl.multiple_of(spot * rows, rows), rows), :] = piece[...]


SCALARS = 8

SMEM = pl.BlockSpec(memory_space=pltpu.SMEM)
VMEM = pl.BlockSpec(memory_space=pltpu.VMEM)


def call(kernel, outs, scratch, scalars, arrays, cost, name, out_specs=None):
    moved = sum(4 * array.size for array in arrays)
    limit = (20 if scratch else 10) * 1024 * 1024
    return pl.pallas_call(
        kernel,
        out_shape=[jax.ShapeDtypeStruct(shape, F32) for shape in outs],
        in_specs=[SMEM] * len(scalars) + [VMEM] * len(arrays),
        out_specs=out_specs or [VMEM] * len(outs),
        scratch_shapes=[pltpu.VMEM(shape, F32) for shape in scratch],
        compiler_params=pltpu.CompilerParams(vmem_limit_bytes=limit),
        cost_estimate=pl.CostEstimate(flops=cost * 10**9, bytes_accessed=moved, transcendentals=0),
        name=name,
    )(*scalars, *arrays)


def swap(value, axis, bit):
    return lax.ppermute(value, axis, [(i, i ^ bit) for i in range(lax.axis_size(axis))])


def swap_next(value, axis):
    odd = range(1, lax.axis_size(axis) - 1, 2)
    return lax.ppermute(value, axis, [pair for i in odd for pair in ((i, i + 1), (i + 1, i))])


def both_swaps(values, axis):
    if axis == "row":
        later = swap_next(values[1], axis)
        return [later, swap(values[0], axis, 1)]
    return [swap(values[0], axis, 1), swap_next(values[1], axis)]


def higher_bits(axis, bit):
    while bit < lax.axis_size(axis):
        yield bit
        bit *= 2


def on_device(object_slices, probe, propagator, measured, positions, scan_counts):
    layers = object_slices.shape[0]
    tile = object_slices.shape[2]
    width = probe.shape[1]
    half = width // 2
    slots = measured.shape[2]
    long = 2 * half + tile
    matrices, turns = (jnp.asarray(value) for value in tables(width))
    transforms = [turns, matrices]
    fields = (slots, 2, width, width)
    side, strip, middle = (2, tile, half), (2, half, long), (2, tile, long)
    wide, one = (2, 3 + tile // half, long, half), (2, width, width)
    two = (2, *one)
    places = jnp.concatenate([positions[0, 0].T, jnp.broadcast_to(scan_counts, (1, slots))], axis=0)

    edges = call(edges_kernel, [side] * (2 * layers), [], [], [object_slices], 0, "tile_edges")
    sides = [both_swaps(edges[2 * at : 2 * at + 2], "col") for at in range(layers)]
    targets, transfer, level_scalars = call(
        prepare_kernel, [(slots, width, width), one, (SCALARS, width)], [], [places],
        [measured[0, 0], propagator, matrices],
        6, "reorder_targets",
    )
    sides[0], targets, transfer = lax.optimization_barrier((sides[0], targets, transfer))
    strips = []
    for at in range(layers):
        pair = call(
            functools.partial(widen_kernel, at), [strip, strip], [], [],
            [object_slices, *sides[at]], 20, "widen",
        )
        strips.append(both_swaps(pair, "row"))

    waves, patches = call(
        first_kernel, [fields, fields], [wide, two], [places],
        [object_slices, *sides[0], *strips[0], probe, transfer, *transforms], 20, "first_slice",
    )
    backs, centre, *ends = call(
        second_kernel, [fields, middle, strip, strip], [wide, wide, two, two], [places],
        [object_slices, *sides[1], *strips[1], waves, targets, *transforms], 20, "second_slice",
    )

    def add_rows(centre, ends, cost=20):
        return call(
            rows_kernel, [(2, tile, tile), side, side], [], [], [centre, *ends], cost, "add_rows"
        )

    def halve(which, kept, received, cost=0):
        half_shape = ((kept.shape[0] - SCALARS) // 2 + SCALARS, width)
        return call(
            functools.partial(halve_kernel, which), [half_shape, half_shape], [], [],
            [kept, received], cost, "halve",
        )

    ends_last, centre_last = both_swaps(ends, "row"), centre
    message = (width + SCALARS, width)
    adjoints, keep, send = call(
        third_kernel, [fields, message, message], [two, one], [places],
        [level_scalars, patches, backs, probe, transfer, *transforms], 20, "first_adjoint",
    )
    centre, *ends = call(
        fourth_kernel, [middle, strip, strip], [wide], [places],
        [probe, adjoints], 0, "first_gradient",
    )
    received, centre, ends = lax.optimization_barrier((swap(send, "row", 1), centre, ends))
    keep, send = halve(2, keep, received)
    send, ends, ends_last = lax.optimization_barrier((send, ends, ends_last))
    ends = both_swaps(ends, "row")
    owned_last, *sides_last = add_rows(centre_last, ends_last)
    sides_last = both_swaps(sides_last, "col")
    keep, send = halve(3, keep, swap(send, "row", 2), 20)
    state = keep + swap(send, "row", 4)
    state, ends, sides_last = lax.optimization_barrier((state, ends, sides_last))
    owned_first, *sides_first = add_rows(centre, ends)
    sides_first = both_swaps(sides_first, "col")
    (state,) = call(
        add_kernel, [state.shape], [], [],
        [state, *(swap(state, "col", bit) for bit in range(1, 4))], 20, "add",
    )
    for axis, bit in (("col", 4), ("row", 8)):
        for bit in higher_bits(axis, bit):
            state = state + swap(state, axis, bit)
    scalars, mine = state[-SCALARS:], state[:-SCALARS]
    (own,) = call(
        join_kernel, [(width, width)], [], [],
        [mine, *(swap(mine, "row", bit) for bit in (4, 2, 6))], 0, "join",
    )
    other = swap(own, "row", 1)
    (object_grad,) = call(
        finish_object_kernel, [object_slices.shape], [], [],
        [scalars, owned_first, *sides_first, owned_last, *sides_last], 20, "finish_object",
    )
    other, object_grad = lax.optimization_barrier((other, object_grad))
    (probe_grad,) = call(finish_probe_kernel, [one], [], [], [scalars, own, other], 0, "finish_probe")
    return object_grad, probe_grad


def solution(mesh):
    placed = (
        P(None, None, "row", "col"),
        P(),
        P(),
        P("row", "col", None, None, None),
        P("row", "col", None, None),
        P("row", "col"),
    )
    return jax.shard_map(
        on_device,
        mesh=mesh,
        in_specs=placed,
        out_specs=(P(None, None, "row", "col"), P()),
        check_vma=False,
    )
```
